256 devices in a mesh: clip: 16 (over z_lo, x), seq: 16 (over y, z_hi, core).
Axes of the slice: x: 4, y: 4, z: 8 (z_hi: 2, z_lo: 4; z = z_hi * 4 + z_lo), core: 2. Of those that a mesh axis runs over, the one named last changes fastest.
Arguments:
- t_query: bfloat16 [16, 4096, 1408], P('clip', 'seq'), may hold values from -8 to 8
- t_key: bfloat16 [16, 4096, 1408], P('clip', 'seq'), may hold values from -8 to 8
- t_value: bfloat16 [16, 4096, 1408], P('clip', 'seq'), may hold values from -6 to 6
- context: bfloat16 [16, 4096, 384], P('clip', 'seq'), may hold values from -6 to 6
- mask_list: int32 [16, 16, 256], P('clip'), may hold values from -1 to 4095, as said below
- block_owner: int32 [16, 16], P('clip'), may hold values from 0 to 15, each once within a row
- p_gain: float32 [384], replicated, may hold values from 0.25 to 1.75
- w_query: bfloat16 [384, 384], replicated, may hold values from -0.3125 to 0.3125
- w_key: bfloat16 [384, 384], replicated, may hold values from -0.3125 to 0.3125
- w_value: bfloat16 [384, 384], replicated, may hold values from -0.3125 to 0.3125
- w_proj: bfloat16 [384, 1408], replicated, may hold values from -0.3125 to 0.3125
Outputs:
- prediction: bfloat16 [16, 4096, 1408], P('clip', 'seq')
- loss: float32 [16], P('clip')
- grad_proj: float32 [384, 1408], P('clip', 'seq')
The draws below stay inside these ranges and needn't reach their ends.
Inputs may be any that keep to these rules, and one draw needn't show every extreme that they name: `mask_list`: in block b of a clip, slots s * 16 to (s + 1) * 16 - 1 hold distinct positions of tokens s * 256 to (s + 1) * 256 - 1, filled slots first, then -1; a position appears at most once in a clip; in every clip one block has all slots filled, and some block has an empty slot; the last token of a clip is masked in every clip.
All inputs are finite; a program needn't handle non-finite values.
Results may differ from the reference program's by a relative error of at most 0.014.
Values may be sent and summed in bfloat16 or wider, within the bound.
No kernel may reach another device: no remote copies, remote signals or barrier semaphores. Data moves between devices by JAX's collectives and lax.ppermute only.
A program may use at most 128 MiB of HBM per device.

```python
import math
import jax
import jax.numpy as jnp
from jax import lax

TARGET_WIDTH = 1408
TARGET_HEADS = 16
PRED_WIDTH = 384
PRED_HEADS = 12
BLOCK_ROWS = 256
TOK_DEV = 256
CLIPS = 16
TOKENS = 4096
N_SEQ = 16


def draw_t_key(key, part):
    key = jax.random.fold_in(key, 1)
    base = jnp.clip(jax.random.normal(key, (CLIPS, TOKENS, TARGET_WIDTH)), -8.0, 8.0)
    return base.astype(jnp.bfloat16)


def draw_t_query(key, part):
    key = jax.random.fold_in(key, 2)
    base = jnp.clip(jax.random.normal(key, (CLIPS, TOKENS, TARGET_WIDTH)), -8.0, 8.0)
    return base.astype(jnp.bfloat16)


def draw_mask_list(key, part):
    key = jax.random.fold_in(key, 3)
    slot_cap = BLOCK_ROWS // N_SEQ

    def one_clip(clip_key):
        key_hot, key_count, key_perm = jax.random.split(clip_key, 3)
        hottest = jax.random.randint(key_hot, (), 0, N_SEQ)
        counts = jax.random.randint(key_count, (N_SEQ, N_SEQ), 0, slot_cap + 1)
        block_ids = jnp.arange(N_SEQ)[:, None]
        source_ids = jnp.arange(N_SEQ)[None, :]
        short = (block_ids == (hottest + 1) % N_SEQ) & (source_ids == 0)
        counts = jnp.where(short, jnp.minimum(counts, slot_cap - 1), counts)
        counts = jnp.where(block_ids == hottest, slot_cap, counts)
        offsets = jnp.cumsum(counts, axis=0) - counts
        orders = jax.vmap(lambda sub_key: jax.random.permutation(sub_key, TOK_DEV))(jax.random.split(key_perm, N_SEQ))
        spot = offsets[hottest, N_SEQ - 1]
        last_row = orders[N_SEQ - 1]
        displaced = last_row[spot]
        last_row = jnp.where(last_row == TOK_DEV - 1, displaced, last_row)
        last_row = last_row.at[spot].set(TOK_DEV - 1)
        orders = orders.at[N_SEQ - 1].set(last_row)
        slot = jnp.arange(slot_cap)
        index = jnp.minimum(offsets[:, :, None] + slot[None, None, :], TOK_DEV - 1)
        source = jnp.broadcast_to(jnp.arange(N_SEQ)[None, :, None], index.shape)
        local = orders[source, index]
        filled = slot[None, None, :] < counts[:, :, None]
        positions = jnp.where(filled, source * TOK_DEV + local, -1)
        return positions.reshape(N_SEQ, BLOCK_ROWS)
    return jax.vmap(one_clip)(jax.random.split(key, CLIPS)).astype(jnp.int32)


def steps_of(stream_key, extent, pieces, least, top_value):
    def one(dim, blocks):
        steps = jax.random.uniform(jax.random.fold_in(jax.random.fold_in(stream_key, 6), dim), (blocks,), jnp.float32, least / len(pieces), top_value / len(pieces))
        return jnp.repeat(jnp.exp(steps), extent[dim] // blocks).reshape((-1,) + (1,) * (len(extent) - dim - 1))

    level = one(*pieces[0])
    for cut in pieces[1:]:
        level = level * one(*cut)
    return level


def bell_draw(stream_key, dims, deviation, most, cuts=(), kind=jnp.bfloat16):
    drawn = jax.random.normal(stream_key, dims, jnp.float32) * deviation
    if len(cuts) > 0:
        drawn = steps_of(stream_key, dims, cuts, -0.22, 0.18) * drawn
    return jnp.clip(drawn, min=-most, max=most).astype(kind)


def setup_inputs(seed: int = 0) -> dict:
    key_list = jax.random.split(jax.random.key(seed), 12)
    t_query = draw_t_query(jax.random.fold_in(key_list[11], 71), 0)
    t_key = draw_t_key(jax.random.fold_in(key_list[11], 71), 0)
    t_value = bell_draw(key_list[2], (CLIPS, TOKENS, TARGET_WIDTH), 1.0, 6.0, ((0, 16), (1, 16)))
    context = bell_draw(key_list[3], (CLIPS, TOKENS, PRED_WIDTH), 1.0, 6.0, ((0, 16), (1, 16)))
    mask_list = draw_mask_list(jax.random.fold_in(key_list[11], 71), 0)
    block_owner = jax.vmap(lambda own: jax.random.permutation(own, N_SEQ))(jax.random.split(key_list[5], CLIPS)).reshape((CLIPS, N_SEQ)).astype(jnp.int32)
    p_gain = jnp.clip(1.0 + 0.15 * jax.random.normal(key_list[6], (PRED_WIDTH,), jnp.float32), 0.25, 1.75)
    w_query = bell_draw(key_list[7], (PRED_WIDTH, PRED_WIDTH), PRED_WIDTH ** -0.5, 0.3125)
    w_key = bell_draw(key_list[8], (PRED_WIDTH, PRED_WIDTH), PRED_WIDTH ** -0.5, 0.3125)
    w_value = bell_draw(key_list[9], (PRED_WIDTH, PRED_WIDTH), PRED_WIDTH ** -0.5, 0.3125)
    w_proj = bell_draw(key_list[10], (PRED_WIDTH, TARGET_WIDTH), PRED_WIDTH ** -0.5, 0.3125)
    return dict(t_query=t_query, t_key=t_key, t_value=t_value, context=context, mask_list=mask_list, block_owner=block_owner, p_gain=p_gain, w_query=w_query, w_key=w_key, w_value=w_value, w_proj=w_proj)


def attend_clip(query, keys, values):
    tokens = query.shape[0]
    head_dim = TARGET_WIDTH // TARGET_HEADS
    factor = 1.0 / math.sqrt(head_dim)
    query_heads = query.reshape(tokens, TARGET_HEADS, head_dim).transpose(1, 0, 2)
    key_heads = keys.reshape(tokens, TARGET_HEADS, head_dim).transpose(1, 0, 2)
    value_heads = values.reshape(tokens, TARGET_HEADS, head_dim).transpose(1, 0, 2)

    def one_head(group):
        head_query, head_key, head_value = group
        scores = jnp.dot(head_query, head_key.T, preferred_element_type=jnp.float32) * factor
        weights = jnp.exp(scores - lax.optimization_barrier(jnp.max(scores, axis=-1, keepdims=True)))
        mixed = jnp.dot(weights.astype(jnp.bfloat16), head_value, preferred_element_type=jnp.float32)
        return mixed / lax.optimization_barrier(jnp.sum(weights, axis=-1, keepdims=True))
    result = lax.map(one_head, (query_heads, key_heads, value_heads))
    return result.transpose(1, 0, 2).reshape(tokens, TARGET_WIDTH).astype(jnp.bfloat16)

def layer_norm(values):
    mean = lax.optimization_barrier(jnp.mean(values, axis=-1, keepdims=True))
    centered = values - mean
    spread = lax.optimization_barrier(jnp.mean(centered * centered, axis=-1, keepdims=True))
    return centered * lax.rsqrt(spread + 1e-06)

def predict(context_rows, target_rows, valid, count, p_gain, w_query, w_key, w_value, w_proj):
    slots = context_rows.shape[0]
    head_dim = PRED_WIDTH // PRED_HEADS
    stream = context_rows.astype(jnp.float32)
    normed = (layer_norm(stream) * p_gain).astype(jnp.bfloat16)
    queries = jnp.dot(normed, w_query, preferred_element_type=jnp.float32).astype(jnp.bfloat16)
    keys = jnp.dot(normed, w_key, preferred_element_type=jnp.float32).astype(jnp.bfloat16)
    values = jnp.dot(normed, w_value, preferred_element_type=jnp.float32).astype(jnp.bfloat16)
    queries = queries.reshape(slots, PRED_HEADS, head_dim).astype(jnp.float32)
    keys = keys.reshape(slots, PRED_HEADS, head_dim).astype(jnp.float32)
    values = values.reshape(slots, PRED_HEADS, head_dim).astype(jnp.float32)
    scores = jnp.einsum('qhd,khd->hqk', queries, keys) / math.sqrt(head_dim)
    scores = jnp.where(valid[None, None, :], scores, jnp.float32(-1e+30))
    weights = jnp.exp(scores - lax.optimization_barrier(jnp.max(scores, axis=-1, keepdims=True)))
    totals = lax.optimization_barrier(jnp.sum(weights, axis=-1))
    rounded = weights.astype(jnp.bfloat16).astype(jnp.float32)
    mixed = jnp.einsum('hqk,khd->qhd', rounded, values) / totals.T[:, :, None]
    hidden = (stream + mixed.reshape(slots, PRED_WIDTH)).astype(jnp.bfloat16)
    pred = jnp.dot(hidden, w_proj, preferred_element_type=jnp.float32)
    goal = layer_norm(target_rows.astype(jnp.float32))
    diff = pred - goal
    keep = valid[:, None]
    magnitude = jnp.abs(diff)
    huber = jnp.where(magnitude < 1.0, 0.5 * diff * diff, magnitude - 0.5)
    partial_value = jnp.sum(jnp.where(keep, huber, 0.0))
    slope = (jnp.where(keep, jnp.clip(diff, -1.0, 1.0), 0.0) / count).astype(jnp.bfloat16)
    pred_out = jnp.where(keep, pred, 0.0).astype(jnp.bfloat16)
    return (pred_out, partial_value, hidden, slope)

def reference(t_query, t_key, t_value, context, mask_list, block_owner, p_gain, w_query, w_key, w_value, w_proj):
    predictions = []
    losses = []
    gradient = jnp.zeros((PRED_WIDTH, TARGET_WIDTH), jnp.float32)
    for clip_index in range(CLIPS):
        target = attend_clip(t_query[clip_index], t_key[clip_index], t_value[clip_index])
        lists = mask_list[clip_index]
        valid = lists >= 0
        safe = jnp.where(valid, lists, 0).astype(jnp.int32)
        count = jnp.sum(valid.astype(jnp.float32))
        target_rows = jnp.where(valid[..., None], target[safe], jnp.zeros((), target.dtype))
        context_rows = jnp.where(valid[..., None], context[clip_index][safe], jnp.zeros((), context.dtype))
        pred_out, partial_value, hidden, slope = jax.vmap(predict, in_axes=(0, 0, 0, None, None, None, None, None, None))(context_rows, target_rows, valid, count, p_gain, w_query, w_key, w_value, w_proj)
        gradient = gradient + jnp.einsum('brp,brt->pt', hidden.astype(jnp.float32), slope.astype(jnp.float32))
        holder = jnp.argsort(block_owner[clip_index])
        predictions.append(pred_out[holder].reshape(N_SEQ * BLOCK_ROWS, TARGET_WIDTH))
        losses.append(jnp.sum(partial_value) / (count * TARGET_WIDTH))
    return (jnp.stack(predictions), jnp.stack(losses), gradient)
```

```python
import functools
import math

import jax
import jax.numpy as jnp
from jax import lax
from jax.experimental import pallas as pl
from jax.experimental.pallas import tpu as pltpu
from jax.sharding import PartitionSpec as P

TARGET_WIDTH = 1408
TARGET_HEADS = 16
HEAD = TARGET_WIDTH // TARGET_HEADS
PRED_WIDTH = 384
PRED_HEADS = 12
PRED_HEAD = PRED_WIDTH // PRED_HEADS
BLOCK_ROWS = 256
TOK = 256
N_SEQ = 16
TOKENS = TOK * N_SEQ
SLOTS = BLOCK_ROWS // N_SEQ
WINDOW = 256
LANES = 128
PIECE = 3 * HEAD
SCALE = math.log2(math.e) / math.sqrt(HEAD)

BF16 = jnp.bfloat16
F32 = jnp.float32


def mm(a, b):
    return jnp.dot(a, b, preferred_element_type=F32)


def mm_nt(a, b):
    return lax.dot_general(a, b, (((1,), (1,)), ((), ())), preferred_element_type=F32)


def iota(shape, dim):
    return lax.broadcasted_iota(jnp.int32, shape, dim)


def one_hot(mask):
    return jnp.where(mask, 1.0, 0.0).astype(BF16)


def spread_row(values, source):
    pick = one_hot(iota((BLOCK_ROWS, BLOCK_ROWS), 0) == source * SLOTS + iota((BLOCK_ROWS, BLOCK_ROWS), 1) % SLOTS)
    wide = mm(values.astype(BF16), pick)
    own = iota((N_SEQ, BLOCK_ROWS), 1) // SLOTS == iota((N_SEQ, BLOCK_ROWS), 0)
    return jnp.sum(jnp.where(own, wide, 0.0), axis=0, keepdims=True)


def earlier():
    return one_hot(iota((BLOCK_ROWS, BLOCK_ROWS), 0) < iota((BLOCK_ROWS, BLOCK_ROWS), 1))


def head_columns(head):
    start = min(head * HEAD // LANES * LANES, TARGET_WIDTH - WINDOW)
    return start, head * HEAD - start


def pack_kernel(me, owner, lists, query, keys, values, context, lists_out, context_out, send):
    for b in range(N_SEQ):
        lists_out[pl.ds(owner[b], 1), :] = lists[b : b + 1, :]
    position = me[0]
    ordered = lists_out[...]
    local = jnp.where(ordered >= 0, ordered - position * TOK, -1).astype(F32)
    owner_of = one_hot(iota((BLOCK_ROWS, N_SEQ), 0) // SLOTS == iota((BLOCK_ROWS, N_SEQ), 1))
    wide = mm(owner_of, local.astype(BF16))
    mine = iota((BLOCK_ROWS, BLOCK_ROWS), 1) == position * SLOTS + iota((BLOCK_ROWS, BLOCK_ROWS), 0) % SLOTS
    column = jnp.sum(jnp.where(mine, wide, 0.0), axis=1, keepdims=True)
    row = spread_row(local, position)
    token = iota((BLOCK_ROWS, TOK), 1).astype(F32)
    gather = one_hot(column == token)
    context_out[...] = mm(gather, context[...]).astype(BF16)
    valid = jnp.broadcast_to(row >= 0, (8, BLOCK_ROWS))
    rank = mm(one_hot(valid), earlier())[0:1]
    rank = jnp.where(row >= 0, rank, -1.0)
    compact = one_hot(rank == iota((BLOCK_ROWS, BLOCK_ROWS), 0).astype(F32))
    compact = mm(compact, gather).astype(BF16)
    packed_query = mm(compact, query[...]).astype(BF16)
    for head in range(TARGET_HEADS):
        start, offset = head_columns(head)
        select = one_hot(iota((HEAD, WINDOW), 1) == iota((HEAD, WINDOW), 0) + offset)
        parts = [
            mm_nt(select, keys[:, start : start + WINDOW]),
            mm_nt(select, values[:, start : start + WINDOW]),
            mm_nt(select, packed_query[:, start : start + WINDOW]),
        ]
        send[head] = jnp.concatenate(parts, axis=0).astype(BF16)


def pack(me, owner, lists, query, keys, values, context):
    smem = pl.BlockSpec(memory_space=pltpu.SMEM)
    vmem = pl.BlockSpec(memory_space=pltpu.VMEM)
    return pl.pallas_call(
        pack_kernel,
        out_shape=(
            jax.ShapeDtypeStruct((N_SEQ, BLOCK_ROWS), jnp.int32),
            jax.ShapeDtypeStruct((BLOCK_ROWS, PRED_WIDTH), BF16),
            jax.ShapeDtypeStruct((TARGET_HEADS, PIECE, TOK), BF16),
        ),
        in_specs=[smem, smem] + [vmem] * 5,
        out_specs=(vmem, vmem, vmem),
        compiler_params=pltpu.CompilerParams(vmem_limit_bytes=40 * 2**20),
        cost_estimate=pl.CostEstimate(flops=3 * 10**9, bytes_accessed=5 * 10**6, transcendentals=0),
    )(me, owner, lists, query, keys, values, context)


def predict_kernel(me, lists, context, gain, w_query, w_key, w_value, w_proj, hidden_out, pred_out, rank_out):
    position = me[0]
    stream = context[...].astype(F32)
    mean = jnp.mean(stream, axis=1, keepdims=True)
    centered = stream - mean
    spread = jnp.mean(centered * centered, axis=1, keepdims=True)
    normed = (centered * lax.rsqrt(spread + 1e-6) * gain[...]).astype(BF16)
    queries = mm(normed, w_query[...]).astype(BF16)
    keys = mm(normed, w_key[...]).astype(BF16)
    values = mm(normed, w_value[...]).astype(BF16)
    key_valid = lists[pl.ds(position, 1), :] >= 0
    square = (BLOCK_ROWS, BLOCK_ROWS)
    diagonal = jnp.where(iota(square, 0) == iota(square, 1), jnp.where(key_valid, 1.0, 0.0), 0.0)
    row_valid = jnp.sum(diagonal, axis=1, keepdims=True) > 0.5
    groups = []
    for group in range(PRED_WIDTH // LANES):
        columns = slice(group * LANES, (group + 1) * LANES)
        total = jnp.zeros((BLOCK_ROWS, LANES), F32)
        for head in range(LANES // PRED_HEAD):
            own = iota((BLOCK_ROWS, LANES), 1) // PRED_HEAD == head
            masked = jnp.where(own, queries[:, columns], jnp.zeros((), BF16))
            scores = mm_nt(masked, keys[:, columns]) * (1.0 / math.sqrt(PRED_HEAD))
            scores = jnp.where(key_valid, scores, -1e30)
            weights = jnp.exp(scores - jnp.max(scores, axis=1, keepdims=True))
            totals = jnp.sum(weights, axis=1, keepdims=True)
            mixed = mm(weights.astype(BF16), values[:, columns]) / totals
            total = total + jnp.where(own, mixed, 0.0)
        groups.append(total)
    hidden = (stream + jnp.concatenate(groups, axis=1)).astype(BF16)
    hidden_out[...] = hidden
    pred = mm(hidden, w_proj[...])
    pred_out[...] = jnp.where(row_valid, pred, 0.0).astype(BF16)
    filled = jnp.where(lists[...] >= 0, 1.0, 0.0)
    rows = jnp.concatenate([spread_row(filled, source) for source in range(N_SEQ)], axis=0)
    rank_out[...] = jnp.where(rows > 0.5, mm(rows.astype(BF16), earlier()), -1.0)


def predict(me, lists, context, gain, w_query, w_key, w_value, w_proj):
    smem = pl.BlockSpec(memory_space=pltpu.SMEM)
    vmem = pl.BlockSpec(memory_space=pltpu.VMEM)
    return pl.pallas_call(
        predict_kernel,
        out_shape=(
            jax.ShapeDtypeStruct((BLOCK_ROWS, PRED_WIDTH), BF16),
            jax.ShapeDtypeStruct((BLOCK_ROWS, TARGET_WIDTH), BF16),
            jax.ShapeDtypeStruct((N_SEQ, BLOCK_ROWS), F32),
        ),
        in_specs=[smem] + [vmem] * 7,
        out_specs=(vmem, vmem, vmem),
        compiler_params=pltpu.CompilerParams(vmem_limit_bytes=40 * 2**20),
        cost_estimate=pl.CostEstimate(flops=3 * 10**9, bytes_accessed=4 * 10**6, transcendentals=10**6),
    )(me, lists, context, gain, w_query, w_key, w_value, w_proj)


ROWS = 256
CHUNK = 1024
PACKED = TOKENS + TOK
LOW, HIGH = 2.0**-80, 2.0**100


def attend_kernel(plan, rank, received, target_out, stats_out, key_t, value, packed, result):
    packed[...] = jnp.zeros((PACKED, LANES), BF16)
    result[...] = jnp.zeros((PACKED, LANES), BF16)
    for source in range(N_SEQ):
        piece = received[source].astype(F32)
        rest = jnp.zeros((LANES - HEAD, TOK), F32)
        key_t[:, source * TOK : (source + 1) * TOK] = jnp.concatenate([piece[:HEAD], rest], axis=0).astype(BF16)
        with_ones = jnp.concatenate([piece[HEAD : 2 * HEAD], rest + 1.0], axis=0)
        value[source * TOK : (source + 1) * TOK, :] = with_ones.T.astype(BF16)
        queries = jnp.concatenate([piece[2 * HEAD :], rest], axis=0).T.astype(BF16)
        packed[pl.ds(pl.multiple_of(plan[source], SLOTS), TOK), :] = queries

    def tile(index, _):
        rows = pl.ds(pl.multiple_of(index * ROWS, ROWS), ROWS)
        query = packed[rows, :]
        total = jnp.zeros((ROWS, LANES), F32)
        for chunk in range(TOKENS // CHUNK):
            span = slice(chunk * CHUNK, (chunk + 1) * CHUNK)
            weights = jnp.exp2(mm(query, key_t[:, span]) * SCALE).astype(BF16)
            total = total + mm(weights, value[span, :])
        sums = total[:, HEAD : HEAD + 1]
        result[rows, :] = (total / sums).astype(BF16)
        safe = (jnp.min(sums) > LOW) & (jnp.max(sums) < HIGH)

        @pl.when(jnp.logical_not(safe))
        def _():
            def peak(chunk, most):
                span = pl.ds(pl.multiple_of(chunk * TOK, TOK), TOK)
                return jnp.maximum(most, jnp.max(mm(query, key_t[:, span]), axis=1, keepdims=True))

            most = lax.fori_loop(0, TOKENS // TOK, peak, jnp.full((ROWS, 1), -1e30, F32))

            def mix(chunk, total):
                span = pl.ds(pl.multiple_of(chunk * TOK, TOK), TOK)
                weights = jnp.exp2((mm(query, key_t[:, span]) - most) * SCALE).astype(BF16)
                return total + mm(weights, value[span, :])

            total = lax.fori_loop(0, TOKENS // TOK, mix, jnp.zeros((ROWS, LANES), F32))
            result[rows, :] = (total / total[:, HEAD : HEAD + 1]).astype(BF16)

        return 0

    lax.fori_loop(0, plan[N_SEQ], tile, 0)

    place = iota((TOK, BLOCK_ROWS), 0).astype(F32)
    for source in range(N_SEQ):
        rows = result[pl.ds(pl.multiple_of(plan[source], SLOTS), TOK), :]
        unpack = one_hot(rank[source : source + 1, :] == place)
        target = mm(rows.astype(F32).T[:HEAD].astype(BF16), unpack)
        target_out[source] = target.astype(BF16)
        mean = jnp.mean(target, axis=0, keepdims=True)
        centered = target - mean
        stats_out[0, source : source + 1, :] = mean
        stats_out[1, source : source + 1, :] = jnp.sum(centered * centered, axis=0, keepdims=True)


def attend(plan, rank, received):
    smem = pl.BlockSpec(memory_space=pltpu.SMEM)
    vmem = pl.BlockSpec(memory_space=pltpu.VMEM)
    return pl.pallas_call(
        attend_kernel,
        out_shape=(
            jax.ShapeDtypeStruct((N_SEQ, HEAD, BLOCK_ROWS), BF16),
            jax.ShapeDtypeStruct((2, N_SEQ, BLOCK_ROWS), F32),
        ),
        in_specs=[smem, vmem, vmem],
        out_specs=(vmem, vmem),
        scratch_shapes=[
            pltpu.VMEM((LANES, TOKENS), BF16),
            pltpu.VMEM((TOKENS, LANES), BF16),
            pltpu.VMEM((PACKED, LANES), BF16),
            pltpu.VMEM((PACKED, LANES), BF16),
        ],
        compiler_params=pltpu.CompilerParams(vmem_limit_bytes=48 * 2**20),
        cost_estimate=pl.CostEstimate(flops=12 * 10**9, bytes_accessed=3 * 10**6, transcendentals=16 * 10**6),
    )(plan, rank, received)


def compare_kernel(me, count, rank, target, stats, hidden, w_proj, grad_out, loss_out):
    position = me[0]
    first = position * HEAD
    start = jnp.minimum(first // LANES * LANES, TARGET_WIDTH - WINDOW)
    window = w_proj[:, pl.ds(pl.multiple_of(start, LANES), WINDOW)]
    select = one_hot(iota((HEAD, WINDOW), 1) == iota((HEAD, WINDOW), 0) + (first - start))
    proj = mm_nt(select, window).astype(BF16)
    means = stats[:, 0]
    mean = jnp.mean(means, axis=0)
    between = means - mean[None]
    spread = (jnp.sum(stats[:, 1], axis=0) + HEAD * jnp.sum(between * between, axis=0)) / TARGET_WIDTH
    scale = lax.rsqrt(spread + 1e-6)
    keep_all = rank[...] >= 0
    share = count[0]
    gradient = jnp.zeros((HEAD, PRED_WIDTH), F32)
    losses = jnp.zeros((HEAD, BLOCK_ROWS), F32)
    for source in range(N_SEQ):
        rows = hidden[:, source * SLOTS : (source + 1) * SLOTS, :].reshape(BLOCK_ROWS, PRED_WIDTH)
        pred = mm_nt(proj, rows)
        one = slice(source, source + 1)
        goal = (target[source].astype(F32) - mean[one]) * scale[one]
        diff = pred - goal
        keep = keep_all[one]
        size = jnp.abs(diff)
        huber = jnp.where(size < 1.0, 0.5 * diff * diff, size - 0.5)
        losses = losses + jnp.where(keep, huber, 0.0)
        slope = jnp.where(keep, jnp.clip(diff, -1.0, 1.0), 0.0) / share
        gradient = gradient + mm(slope.astype(BF16), rows)
    rest = jnp.zeros((LANES - HEAD, PRED_WIDTH), F32)
    grad_out[...] = jnp.concatenate([gradient, rest], axis=0).T
    loss_out[...] = jnp.broadcast_to(jnp.sum(losses), (8, LANES))


def compare(me, count, rank, target, stats, hidden, w_proj):
    smem = pl.BlockSpec(memory_space=pltpu.SMEM)
    vmem = pl.BlockSpec(memory_space=pltpu.VMEM)
    return pl.pallas_call(
        compare_kernel,
        out_shape=(
            jax.ShapeDtypeStruct((PRED_WIDTH, LANES), F32),
            jax.ShapeDtypeStruct((8, LANES), F32),
        ),
        in_specs=[smem, smem] + [vmem] * 5,
        out_specs=(vmem, vmem),
        compiler_params=pltpu.CompilerParams(vmem_limit_bytes=48 * 2**20),
        cost_estimate=pl.CostEstimate(flops=10**9, bytes_accessed=5 * 10**6, transcendentals=0),
    )(me, count, rank, target, stats, hidden, w_proj)


def exchange(pieces, axis):
    return lax.all_to_all(pieces, axis, split_axis=0, concat_axis=0, tiled=True)


def body(
    t_query, t_key, t_value, context, mask_list, block_owner, p_gain, w_query, w_key, w_value, w_proj
):
    me = lax.axis_index("seq").astype(jnp.int32).reshape(1)
    lists, context_rows, send = pack(
        me, block_owner[0], mask_list[0], t_query[0], t_key[0], t_value[0], context[0]
    )
    got_context = exchange(context_rows.reshape(N_SEQ, SLOTS, PRED_WIDTH), "seq")
    received = exchange(send, "seq")
    filled = (mask_list[0] >= 0).astype(jnp.int32)
    per_source = jnp.sum(filled.reshape(N_SEQ, N_SEQ, SLOTS), axis=(0, 2))
    count = jnp.sum(per_source).astype(F32).reshape(1)
    padded = (per_source + SLOTS - 1) // SLOTS * SLOTS
    upper = jnp.arange(N_SEQ)[:, None] < jnp.arange(N_SEQ + 1)[None, :]
    starts = jnp.sum(jnp.where(upper, padded[:, None], 0), axis=0)
    last = jnp.arange(N_SEQ + 1) == N_SEQ
    plan = jnp.where(last, (starts + ROWS - 1) // ROWS, starts).astype(jnp.int32)
    hidden, pred_out, rank = predict(
        me,
        lists,
        got_context.reshape(BLOCK_ROWS, PRED_WIDTH),
        p_gain.reshape(1, PRED_WIDTH),
        w_query,
        w_key,
        w_value,
        w_proj,
    )
    all_hidden = lax.all_gather(hidden, "seq", axis=0)
    target, stats = attend(plan, rank, received)
    stats = exchange(jnp.broadcast_to(stats[None], (N_SEQ,) + stats.shape), "seq")
    gradient, loss = compare(me, count, rank, target, stats, all_hidden, w_proj)
    loss = exchange(jnp.broadcast_to(loss[None], (N_SEQ,) + loss.shape), "seq")
    loss = jnp.sum(loss[:, 0, 0]) / (count * TARGET_WIDTH)
    shares = exchange(gradient.reshape(N_SEQ, PRED_WIDTH // N_SEQ, LANES), "clip")
    gradient = jnp.sum(shares, axis=0)[:, :HEAD]
    return (pred_out[None], loss, gradient)


def solution(mesh):
    in_specs = (
        P("clip", "seq", None),
        P("clip", "seq", None),
        P("clip", "seq", None),
        P("clip", "seq", None),
        P("clip", None, None),
        P("clip", None),
        P(),
        P(),
        P(),
        P(),
        P(),
    )
    out_specs = (P("clip", "seq", None), P("clip"), P("clip", "seq"))
    return jax.shard_map(body, mesh=mesh, in_specs=in_specs, out_specs=out_specs, check_vma=False)
```

```python
import math

import jax
import jax.numpy as jnp
from jax import lax
from jax.experimental import pallas as pl
from jax.experimental.pallas import tpu as pltpu
from jax.sharding import PartitionSpec as P

TARGET_WIDTH = 1408
TARGET_HEADS = 16
HEAD = TARGET_WIDTH // TARGET_HEADS
PRED_WIDTH = 384
PRED_HEADS = 12
PRED_HEAD = PRED_WIDTH // PRED_HEADS
BLOCK_ROWS = 256
TOK = 256
N_SEQ = 16
TOKENS = TOK * N_SEQ
SLOTS = BLOCK_ROWS // N_SEQ
WINDOW = 256
LANES = 128
PIECE = 3 * HEAD
SCALE = math.log2(math.e) / math.sqrt(HEAD)
PRED_SCALE = math.log2(math.e) / math.sqrt(PRED_HEAD)

BF16 = jnp.bfloat16
F32 = jnp.float32


def mm(a, b):
    return jnp.dot(a, b, preferred_element_type=F32)


def mm_nt(a, b):
    return lax.dot_general(a, b, (((1,), (1,)), ((), ())), preferred_element_type=F32)


def iota(shape, dim):
    return lax.broadcasted_iota(jnp.int32, shape, dim)


def one_hot(mask):
    return jnp.where(mask, 1.0, 0.0).astype(BF16)


def spread_row(values, source):
    pick = one_hot(iota((BLOCK_ROWS, BLOCK_ROWS), 0) == source * SLOTS + iota((BLOCK_ROWS, BLOCK_ROWS), 1) % SLOTS)
    wide = mm(values.astype(BF16), pick)
    own = iota((N_SEQ, BLOCK_ROWS), 1) // SLOTS == iota((N_SEQ, BLOCK_ROWS), 0)
    return jnp.sum(jnp.where(own, wide, 0.0), axis=0, keepdims=True)


def earlier():
    return one_hot(iota((BLOCK_ROWS, BLOCK_ROWS), 0) < iota((BLOCK_ROWS, BLOCK_ROWS), 1))


def head_columns(head):
    start = min(head * HEAD // LANES * LANES, TARGET_WIDTH - WINDOW)
    return start, head * HEAD - start


def sender(piece, position):
    step = (position // 4 + 4 - piece // 4) % 4
    return step * 4 + ((position % 4) ^ (piece % 4))


def pack_kernel(me, owner, lists_in, query_in, keys_in, values_in, lists_out, send, lists, query, keys, values, sems):
    loads = [
        pltpu.make_async_copy(source, place, sems.at[i])
        for i, (source, place) in enumerate(
            [(lists_in, lists), (keys_in, keys), (values_in, values), (query_in, query)]
        )
    ]
    for load in loads:
        load.start()
    position = me[0]
    loads[0].wait()
    for b in range(N_SEQ):
        lists_out[pl.ds(owner[0, b], 1), :] = lists[b : b + 1, :]
    ordered = lists_out[...]
    row = spread_row(jnp.where(ordered >= 0, ordered - position * TOK, -1).astype(F32), position)
    valid = jnp.broadcast_to(row >= 0, (8, BLOCK_ROWS))
    rank = mm(one_hot(valid), earlier())[0:1]
    rank = jnp.where(row >= 0, rank, -1.0)
    place = iota((BLOCK_ROWS, BLOCK_ROWS), 0).astype(F32)
    compact = mm_nt(one_hot(rank == place), one_hot(row == place)).astype(BF16)
    for load in loads[1:]:
        load.wait()
    packed_query = mm(compact, query[...]).astype(BF16)
    for head in range(TARGET_HEADS):
        start, offset = head_columns(head)
        select = one_hot(iota((HEAD, WINDOW), 1) == iota((HEAD, WINDOW), 0) + offset)
        parts = [
            mm_nt(select, keys[:, start : start + WINDOW]),
            mm_nt(select, values[:, start : start + WINDOW]),
            mm_nt(select, packed_query[:, start : start + WINDOW]),
        ]
        send[head] = jnp.concatenate(parts, axis=0).astype(BF16)


def pack(me, owner, lists, query, keys, values):
    smem = pl.BlockSpec(memory_space=pltpu.SMEM)
    vmem = pl.BlockSpec(memory_space=pltpu.VMEM)
    hbm = pl.BlockSpec(memory_space=pltpu.HBM)
    return pl.pallas_call(
        pack_kernel,
        out_shape=(
            jax.ShapeDtypeStruct((N_SEQ, BLOCK_ROWS), jnp.int32),
            jax.ShapeDtypeStruct((TARGET_HEADS, PIECE, TOK), BF16),
        ),
        in_specs=[smem, smem] + [hbm] * 4,
        out_specs=(vmem, vmem),
        scratch_shapes=[
            pltpu.VMEM((N_SEQ, BLOCK_ROWS), jnp.int32),
            pltpu.VMEM((TOK, TARGET_WIDTH), BF16),
            pltpu.VMEM((TOK, TARGET_WIDTH), BF16),
            pltpu.VMEM((TOK, TARGET_WIDTH), BF16),
            pltpu.SemaphoreType.DMA((4,)),
        ],
        compiler_params=pltpu.CompilerParams(vmem_limit_bytes=56 * 2**20),
        cost_estimate=pl.CostEstimate(flops=3 * 10**9, bytes_accessed=5 * 10**6, transcendentals=0),
    )(me, owner, lists, query, keys, values)


def rank_kernel(lists, rank_out, local_out):
    ordered = lists[...]
    rows = []
    for source in range(N_SEQ):
        local = jnp.where(ordered >= 0, ordered - source * TOK, -1).astype(F32)
        rows.append(spread_row(local, source))
    local = jnp.concatenate(rows, axis=0)
    rank_out[...] = jnp.where(local >= 0, mm(one_hot(local >= 0), earlier()), -1.0)
    local_out[...] = jnp.concatenate([local, jnp.zeros((LANES - N_SEQ, BLOCK_ROWS), F32)], axis=0).T


def ranks(lists):
    vmem = pl.BlockSpec(memory_space=pltpu.VMEM)
    return pl.pallas_call(
        rank_kernel,
        out_shape=(
            jax.ShapeDtypeStruct((N_SEQ, BLOCK_ROWS), F32),
            jax.ShapeDtypeStruct((BLOCK_ROWS, LANES), F32),
        ),
        in_specs=[vmem],
        out_specs=(vmem, vmem),
        compiler_params=pltpu.CompilerParams(vmem_limit_bytes=8 * 2**20),
        cost_estimate=pl.CostEstimate(flops=10**9, bytes_accessed=10**5, transcendentals=0),
    )(lists)


def arrange_kernel(me, local, context, beyond, rows_out):
    for over, source in enumerate((context, beyond)):
        own = iota((BLOCK_ROWS, LANES), 1) == (me[0] ^ (2 * over))
        column = jnp.sum(jnp.where(own, local[...], 0.0), axis=1, keepdims=True)
        gather = one_hot(column == iota((BLOCK_ROWS, TOK), 1).astype(F32))
        rows_out[over] = mm(gather, source[...]).astype(BF16)


def arrange(me, local, context, beyond):
    smem = pl.BlockSpec(memory_space=pltpu.SMEM)
    vmem = pl.BlockSpec(memory_space=pltpu.VMEM)
    return pl.pallas_call(
        arrange_kernel,
        out_shape=jax.ShapeDtypeStruct((2, BLOCK_ROWS, PRED_WIDTH), BF16),
        in_specs=[smem] + [vmem] * 3,
        out_specs=vmem,
        compiler_params=pltpu.CompilerParams(vmem_limit_bytes=8 * 2**20),
        cost_estimate=pl.CostEstimate(flops=2 * 10**8, bytes_accessed=10**6, transcendentals=0),
    )(me, local, context, beyond)


def predict_kernel(me, lists, *refs):
    pieces = refs[:8]
    gain, w_query, w_key, w_value, hidden_out, context = refs[8:]
    position = me[0]
    for index in range(8):
        for over in range(2):
            source = sender((index % 4) * 4 + over * 2 + index // 4, position)
            rows = pieces[index][over].reshape(N_SEQ, SLOTS, PRED_WIDTH)
            context[:, pl.ds(pl.multiple_of(source * SLOTS, SLOTS), SLOTS), :] = rows

    def block(index, _):
        own = 2 * index + position % 2
        stream = context[own].astype(F32)
        mean = jnp.mean(stream, axis=1, keepdims=True)
        centered = stream - mean
        spread = jnp.mean(centered * centered, axis=1, keepdims=True)
        normed = (centered * lax.rsqrt(spread + 1e-6) * gain[...]).astype(BF16)
        queries = mm(normed, w_query[...]).astype(BF16)
        keys = mm(normed, w_key[...]).astype(BF16)
        values = mm(normed, w_value[...]).astype(BF16)
        key_valid = lists[pl.ds(own, 1), :] >= 0
        ones = jnp.ones((BLOCK_ROWS, LANES), BF16)
        groups = []
        for group in range(PRED_WIDTH // LANES):
            columns = slice(group * LANES, (group + 1) * LANES)
            with_ones = jnp.concatenate([values[:, columns], ones], axis=1)
            total = jnp.zeros((BLOCK_ROWS, LANES), F32)
            sums = jnp.ones((BLOCK_ROWS, LANES), F32)
            for head in range(LANES // PRED_HEAD):
                inside = iota((BLOCK_ROWS, LANES), 1) // PRED_HEAD == head
                masked = jnp.where(inside, queries[:, columns], jnp.zeros((), BF16))
                scores = jnp.where(key_valid, mm_nt(masked, keys[:, columns]), -1e30)
                most = jnp.max(scores, axis=1, keepdims=True)
                weights = jnp.exp2((scores - most) * PRED_SCALE)
                mixed = mm(weights.astype(BF16), with_ones)
                total = jnp.where(inside, mixed[:, :LANES], total)
                sums = jnp.where(inside, mixed[:, LANES:], sums)
            groups.append(total / sums)
        hidden_out[index] = (stream + jnp.concatenate(groups, axis=1)).astype(BF16)
        return 0

    lax.fori_loop(0, N_SEQ // 2, block, 0)


def predict(me, lists, pieces, gain, w_query, w_key, w_value):
    smem = pl.BlockSpec(memory_space=pltpu.SMEM)
    vmem = pl.BlockSpec(memory_space=pltpu.VMEM)
    return pl.pallas_call(
        predict_kernel,
        out_shape=jax.ShapeDtypeStruct((N_SEQ // 2, BLOCK_ROWS, PRED_WIDTH), BF16),
        in_specs=[smem] + [vmem] * 13,
        out_specs=vmem,
        scratch_shapes=[pltpu.VMEM((N_SEQ, BLOCK_ROWS, PRED_WIDTH), BF16)],
        compiler_params=pltpu.CompilerParams(vmem_limit_bytes=16 * 2**20),
        cost_estimate=pl.CostEstimate(flops=13 * 10**9, bytes_accessed=8 * 10**6, transcendentals=10**7),
    )(me, lists, *pieces, gain, w_query, w_key, w_value)


def project_kernel(me, lists, hidden, w_proj, pred_out):
    key_valid = lists[pl.ds(me[0], 1), :] >= 0
    square = (BLOCK_ROWS, BLOCK_ROWS)
    diagonal = jnp.where(iota(square, 0) == iota(square, 1), jnp.where(key_valid, 1.0, 0.0), 0.0)
    row_valid = jnp.sum(diagonal, axis=1, keepdims=True) > 0.5
    pred_out[...] = jnp.where(row_valid, mm(hidden[me[0] // 2], w_proj[...]), 0.0).astype(BF16)


def project(me, lists, hidden, w_proj):
    smem = pl.BlockSpec(memory_space=pltpu.SMEM)
    vmem = pl.BlockSpec(memory_space=pltpu.VMEM)
    return pl.pallas_call(
        project_kernel,
        out_shape=jax.ShapeDtypeStruct((BLOCK_ROWS, TARGET_WIDTH), BF16),
        in_specs=[smem] + [vmem] * 3,
        out_specs=vmem,
        compiler_params=pltpu.CompilerParams(vmem_limit_bytes=8 * 2**20),
        cost_estimate=pl.CostEstimate(flops=3 * 10**8, bytes_accessed=10**6, transcendentals=0),
    )(me, lists, hidden, w_proj)


ROWS = 256
CHUNK = 1024
PACKED = TOKENS + TOK
LOW, HIGH = 2.0**-80, 2.0**100


def attend_tile(index, query_rows, key_t, value, result):
    rows = pl.ds(pl.multiple_of(index * ROWS, ROWS), ROWS)
    query = query_rows[rows, :]
    total = jnp.zeros((ROWS, LANES), F32)
    for chunk in range(TOKENS // CHUNK):
        span = slice(chunk * CHUNK, (chunk + 1) * CHUNK)
        weights = jnp.exp2(mm(query, key_t[:, span]) * SCALE).astype(BF16)
        total = total + mm(weights, value[span, :])
    sums = total[:, HEAD : HEAD + 1]
    result[rows, :] = (total / sums).astype(BF16)
    safe = (jnp.min(sums) > LOW) & (jnp.max(sums) < HIGH)

    @pl.when(jnp.logical_not(safe))
    def _():
        def peak(chunk, most):
            span = pl.ds(pl.multiple_of(chunk * TOK, TOK), TOK)
            return jnp.maximum(most, jnp.max(mm(query, key_t[:, span]), axis=1, keepdims=True))

        most = lax.fori_loop(0, TOKENS // TOK, peak, jnp.full((ROWS, 1), -1e30, F32))

        def mix(chunk, total):
            span = pl.ds(pl.multiple_of(chunk * TOK, TOK), TOK)
            weights = jnp.exp2((mm(query, key_t[:, span]) - most) * SCALE).astype(BF16)
            return total + mm(weights, value[span, :])

        total = lax.fori_loop(0, TOKENS // TOK, mix, jnp.zeros((ROWS, LANES), F32))
        result[rows, :] = (total / total[:, HEAD : HEAD + 1]).astype(BF16)


def attend_kernel(plan, rank, received, target_out, stats_out, key_t, value, packed, result, stats):
    packed[...] = jnp.zeros((PACKED, LANES), BF16)
    result[...] = jnp.zeros((PACKED, LANES), BF16)
    for source in range(N_SEQ):
        piece = received[source].astype(F32)
        rest = jnp.zeros((LANES - HEAD, TOK), F32)
        key_t[:, source * TOK : (source + 1) * TOK] = jnp.concatenate([piece[:HEAD], rest], axis=0).astype(BF16)
        with_ones = jnp.concatenate([piece[HEAD : 2 * HEAD], rest + 1.0], axis=0)
        value[source * TOK : (source + 1) * TOK, :] = with_ones.T.astype(BF16)
        queries = jnp.concatenate([piece[2 * HEAD :], rest], axis=0).T.astype(BF16)
        packed[pl.ds(pl.multiple_of(plan[source], SLOTS), TOK), :] = queries

    def tile(index, _):
        attend_tile(index, packed, key_t, value, result)
        return 0

    lax.fori_loop(0, plan[N_SEQ], tile, 0)
    place = iota((TOK, BLOCK_ROWS), 0).astype(F32)
    for source in range(N_SEQ):
        rows = result[pl.ds(pl.multiple_of(plan[source], SLOTS), TOK), :]
        unpack = one_hot(rank[source : source + 1, :] == place)
        target = lax.dot_general(rows, unpack, (((0,), (0,)), ((), ())), preferred_element_type=F32)[:HEAD]
        target_out[source] = target.astype(BF16)
        mean = jnp.mean(target, axis=0, keepdims=True)
        centered = target - mean
        stats[0, source : source + 1, :] = mean
        stats[1, source : source + 1, :] = jnp.sum(centered * centered, axis=0, keepdims=True)
    for other in range(TARGET_HEADS):
        stats_out[other] = stats[...]


def attend(plan, rank, received):
    smem = pl.BlockSpec(memory_space=pltpu.SMEM)
    vmem = pl.BlockSpec(memory_space=pltpu.VMEM)
    return pl.pallas_call(
        attend_kernel,
        out_shape=(
            jax.ShapeDtypeStruct((N_SEQ, HEAD, BLOCK_ROWS), BF16),
            jax.ShapeDtypeStruct((TARGET_HEADS, 2, N_SEQ, BLOCK_ROWS), F32),
        ),
        in_specs=[smem, vmem, vmem],
        out_specs=(vmem, vmem),
        scratch_shapes=[
            pltpu.VMEM((LANES, TOKENS), BF16),
            pltpu.VMEM((TOKENS, LANES), BF16),
            pltpu.VMEM((PACKED, LANES), BF16),
            pltpu.VMEM((PACKED, LANES), BF16),
            pltpu.VMEM((2, N_SEQ, BLOCK_ROWS), F32),
        ],
        compiler_params=pltpu.CompilerParams(vmem_limit_bytes=16 * 2**20),
        cost_estimate=pl.CostEstimate(flops=12 * 10**9, bytes_accessed=3 * 10**6, transcendentals=16 * 10**6),
    )(plan, rank, received)


def slot_rows(hidden, source):
    span = slice(source * SLOTS, (source + 1) * SLOTS)
    return hidden[:, span, :].reshape(BLOCK_ROWS, PRED_WIDTH)


def compare_kernel(me, count, rank, target, stats, mine, other, w_proj, slope_out, loss_out, hidden):
    position = me[0]
    for index in range(N_SEQ // 2):
        hidden[2 * index + position % 2] = mine[index]
        hidden[2 * index + 1 - position % 2] = other[index]
    first = position * HEAD
    start = jnp.minimum(first // LANES * LANES, TARGET_WIDTH - WINDOW)
    window = w_proj[:, pl.ds(pl.multiple_of(start, LANES), WINDOW)]
    select = one_hot(iota((HEAD, WINDOW), 1) == iota((HEAD, WINDOW), 0) + (first - start))
    proj = mm_nt(select, window).astype(BF16)
    means = stats[:, 0]
    mean = jnp.mean(means, axis=0)
    between = means - mean[None]
    spread = (jnp.sum(stats[:, 1], axis=0) + HEAD * jnp.sum(between * between, axis=0)) / TARGET_WIDTH
    scale = lax.rsqrt(spread + 1e-6)
    keep_all = rank[...] >= 0
    share = 1.0 / jnp.full((1, BLOCK_ROWS), count[0], F32)
    losses = jnp.zeros((HEAD, BLOCK_ROWS), F32)
    for source in range(N_SEQ):
        rows = slot_rows(hidden, source)
        pred = mm_nt(proj, rows)
        one = slice(source, source + 1)
        goal = (target[source].astype(F32) - mean[one]) * scale[one]
        diff = pred - goal
        keep = keep_all[one]
        size = jnp.abs(diff)
        huber = jnp.where(size < 1.0, 0.5 * diff * diff, size - 0.5)
        losses = losses + jnp.where(keep, huber, 0.0)
        slope = jnp.where(keep, jnp.clip(diff, -1.0, 1.0) * share, 0.0)
        slope_out[source] = slope.astype(BF16)
    loss_out[...] = jnp.broadcast_to(jnp.sum(losses), (8, LANES))


def compare(me, count, rank, target, stats, mine, other, w_proj):
    smem = pl.BlockSpec(memory_space=pltpu.SMEM)
    vmem = pl.BlockSpec(memory_space=pltpu.VMEM)
    return pl.pallas_call(
        compare_kernel,
        out_shape=(
            jax.ShapeDtypeStruct((N_SEQ, HEAD, BLOCK_ROWS), BF16),
            jax.ShapeDtypeStruct((8, LANES), F32),
            jax.ShapeDtypeStruct((N_SEQ, BLOCK_ROWS, PRED_WIDTH), BF16),
        ),
        in_specs=[smem, smem] + [vmem] * 6,
        out_specs=(vmem, vmem, vmem),
        compiler_params=pltpu.CompilerParams(vmem_limit_bytes=12 * 2**20),
        cost_estimate=pl.CostEstimate(flops=10**9, bytes_accessed=5 * 10**6, transcendentals=0),
    )(me, count, rank, target, stats, mine, other, w_proj)


def gradient_kernel(slope, hidden, grad_out):
    gradient = jnp.zeros((HEAD, PRED_WIDTH), F32)
    for source in range(N_SEQ):
        rows = slot_rows(hidden, source)
        gradient = gradient + mm(slope[source], rows)
    rest = jnp.zeros((LANES - HEAD, PRED_WIDTH), F32)
    grad_out[...] = jnp.concatenate([gradient, rest], axis=0).T


def project_gradient(slope, hidden):
    vmem = pl.BlockSpec(memory_space=pltpu.VMEM)
    return pl.pallas_call(
        gradient_kernel,
        out_shape=jax.ShapeDtypeStruct((PRED_WIDTH, LANES), F32),
        in_specs=[vmem] * 2,
        out_specs=vmem,
        compiler_params=pltpu.CompilerParams(vmem_limit_bytes=8 * 2**20),
        cost_estimate=pl.CostEstimate(flops=4 * 10**9, bytes_accessed=4 * 10**6, transcendentals=0),
    )(slope, hidden)


def exchange(pieces, axis):
    return lax.all_to_all(pieces, axis, split_axis=0, concat_axis=0, tiled=True)


def across(values, mask):
    return lax.ppermute(values, "seq", [(i, i ^ mask) for i in range(N_SEQ)])


def along(values, step):
    return lax.ppermute(values, "seq", [(i, (i + 4 * step) % N_SEQ) for i in range(N_SEQ)])


def body(
    t_query, t_key, t_value, context, mask_list, block_owner, p_gain, w_query, w_key, w_value, w_proj
):
    me = lax.axis_index("seq").astype(jnp.int32).reshape(1)
    beyond = across(context[0], 2)
    lists, send = pack(me, block_owner, mask_list[0], t_query[0], t_key[0], t_value[0])
    send, beyond = lax.optimization_barrier((send, beyond))
    received = exchange(send, "seq")
    rank, local = ranks(lists)
    pair = arrange(me, local, context[0], beyond)
    column = [pair] + [along(pair, step) for step in range(1, 4)]
    pieces = column + [across(part, 1) for part in column]
    filled = (mask_list[0] >= 0).astype(jnp.int32)
    per_source = jnp.sum(filled.reshape(N_SEQ, N_SEQ, SLOTS), axis=(0, 2))
    count = jnp.sum(per_source).astype(F32).reshape(1)
    padded = (per_source + SLOTS - 1) // SLOTS * SLOTS
    upper = jnp.arange(N_SEQ)[:, None] < jnp.arange(N_SEQ + 1)[None, :]
    starts = jnp.sum(jnp.where(upper, padded[:, None], 0), axis=0)
    last = jnp.arange(N_SEQ + 1) == N_SEQ
    plan = jnp.where(last, (starts + ROWS - 1) // ROWS, starts).astype(jnp.int32)
    hidden = predict(me, lists, pieces, p_gain.reshape(1, PRED_WIDTH), w_query, w_key, w_value)
    received, hidden = lax.optimization_barrier((received, hidden))
    others = across(hidden, 1)
    target, stats = attend(plan, rank, received)
    stats = exchange(stats, "seq")
    pred_out = project(me, lists, hidden, w_proj)
    slope, loss, rows = compare(me, count, rank, target, stats, hidden, others, w_proj)
    loss, slope = lax.optimization_barrier((loss, slope))
    loss = loss + across(loss, 2)
    gradient = project_gradient(slope, rows)
    loss, gradient = lax.optimization_barrier((loss, gradient))
    shares = exchange(gradient.reshape(N_SEQ, PRED_WIDTH // N_SEQ, LANES), "clip")
    for mask in (1, 4, 8):
        loss = loss + across(loss, mask)
    loss = loss[0, :1] / (count * TARGET_WIDTH)
    gradient = jnp.sum(shares, axis=0)[:, :HEAD]
    return (pred_out[None], loss, gradient)


def solution(mesh):
    in_specs = (
        P("clip", "seq", None),
        P("clip", "seq", None),
        P("clip", "seq", None),
        P("clip", "seq", None),
        P("clip", None, None),
        P("clip", None),
        P(),
        P(),
        P(),
        P(),
        P(),
    )
    out_specs = (P("clip", "seq", None), P("clip"), P("clip", "seq"))
    return jax.shard_map(body, mesh=mesh, in_specs=in_specs, out_specs=out_specs, check_vma=False)
```

```python
import math

import jax
import jax.numpy as jnp
from jax import lax
from jax.experimental import pallas as pl
from jax.experimental.pallas import tpu as pltpu
from jax.sharding import PartitionSpec as P

TARGET_WIDTH = 1408
TARGET_HEADS = 16
HEAD = TARGET_WIDTH // TARGET_HEADS
PRED_WIDTH = 384
PRED_HEADS = 12
PRED_HEAD = PRED_WIDTH // PRED_HEADS
BLOCK_ROWS = 256
TOK = 256
N_SEQ = 16
TOKENS = TOK * N_SEQ
SLOTS = BLOCK_ROWS // N_SEQ
WINDOW = 256
LANES = 128
PIECE = 3 * HEAD
SCALE = math.log2(math.e) / math.sqrt(HEAD)
PRED_SCALE = math.log2(math.e) / math.sqrt(PRED_HEAD)

BF16 = jnp.bfloat16
F32 = jnp.float32


def mm(a, b):
    return jnp.dot(a, b, preferred_element_type=F32)


def mm_nt(a, b):
    return lax.dot_general(a, b, (((1,), (1,)), ((), ())), preferred_element_type=F32)


def iota(shape, dim):
    return lax.broadcasted_iota(jnp.int32, shape, dim)


def one_hot(mask):
    return jnp.where(mask, 1.0, 0.0).astype(BF16)


def spread_row(values, source):
    pick = one_hot(iota((BLOCK_ROWS, BLOCK_ROWS), 0) == source * SLOTS + iota((BLOCK_ROWS, BLOCK_ROWS), 1) % SLOTS)
    wide = mm(values.astype(BF16), pick)
    own = iota((N_SEQ, BLOCK_ROWS), 1) // SLOTS == iota((N_SEQ, BLOCK_ROWS), 0)
    return jnp.sum(jnp.where(own, wide, 0.0), axis=0, keepdims=True)


def earlier():
    return one_hot(iota((BLOCK_ROWS, BLOCK_ROWS), 0) < iota((BLOCK_ROWS, BLOCK_ROWS), 1))


def head_columns(head):
    start = min(head * HEAD // LANES * LANES, TARGET_WIDTH - WINDOW)
    return start, head * HEAD - start


def sender(piece, position):
    step = (position // 4 + 4 - piece // 4) % 4
    return step * 4 + ((position % 4) ^ (piece % 4))


def pack_kernel(me, owner, lists_in, query_in, keys_in, values_in, send, lists, blocks, query, keys, values, sems):
    loads = [
        pltpu.make_async_copy(source, place, sems.at[i])
        for i, (source, place) in enumerate(
            [(lists_in, lists), (keys_in, keys), (values_in, values), (query_in, query)]
        )
    ]
    for load in loads:
        load.start()
    position = me[0]
    loads[0].wait()
    for b in range(N_SEQ):
        blocks[pl.ds(owner[0, b], 1), :] = lists[b : b + 1, :]
    ordered = blocks[...]
    row = spread_row(jnp.where(ordered >= 0, ordered - position * TOK, -1).astype(F32), position)
    valid = jnp.broadcast_to(row >= 0, (8, BLOCK_ROWS))
    rank = mm(one_hot(valid), earlier())[0:1]
    rank = jnp.where(row >= 0, rank, -1.0)
    place = iota((BLOCK_ROWS, BLOCK_ROWS), 0).astype(F32)
    compact = mm_nt(one_hot(rank == place), one_hot(row == place)).astype(BF16)
    for load in loads[1:]:
        load.wait()
    packed_query = mm(compact, query[...]).astype(BF16)
    for head in range(TARGET_HEADS):
        start, offset = head_columns(head)
        select = one_hot(iota((HEAD, WINDOW), 1) == iota((HEAD, WINDOW), 0) + offset)
        parts = [
            mm_nt(select, keys[:, start : start + WINDOW]),
            mm_nt(select, values[:, start : start + WINDOW]),
            mm_nt(select, packed_query[:, start : start + WINDOW]),
        ]
        send[head] = jnp.concatenate(parts, axis=0).astype(BF16)


def pack(me, owner, lists, query, keys, values):
    smem = pl.BlockSpec(memory_space=pltpu.SMEM)
    vmem = pl.BlockSpec(memory_space=pltpu.VMEM)
    hbm = pl.BlockSpec(memory_space=pltpu.HBM)
    return pl.pallas_call(
        pack_kernel,
        out_shape=jax.ShapeDtypeStruct((TARGET_HEADS, PIECE, TOK), BF16),
        in_specs=[smem, smem] + [hbm] * 4,
        out_specs=vmem,
        scratch_shapes=[
            pltpu.VMEM((N_SEQ, BLOCK_ROWS), jnp.int32),
            pltpu.VMEM((N_SEQ, BLOCK_ROWS), jnp.int32),
            pltpu.VMEM((TOK, TARGET_WIDTH), BF16),
            pltpu.VMEM((TOK, TARGET_WIDTH), BF16),
            pltpu.VMEM((TOK, TARGET_WIDTH), BF16),
            pltpu.SemaphoreType.DMA((4,)),
        ],
        compiler_params=pltpu.CompilerParams(vmem_limit_bytes=56 * 2**20),
        cost_estimate=pl.CostEstimate(flops=3 * 10**9, bytes_accessed=5 * 10**6, transcendentals=0),
    )(me, owner, lists, query, keys, values)


def rank_kernel(owner, lists, lists_out, rank_out, local_out, plan_out, count_out):
    for b in range(N_SEQ):
        lists_out[pl.ds(owner[0, b], 1), :] = lists[b : b + 1, :]
    ordered = lists_out[...]
    rows = []
    for source in range(N_SEQ):
        local = jnp.where(ordered >= 0, ordered - source * TOK, -1).astype(F32)
        rows.append(spread_row(local, source))
    local = jnp.concatenate(rows, axis=0)
    rank_out[...] = jnp.where(local >= 0, mm(one_hot(local >= 0), earlier()), -1.0)
    local_out[...] = jnp.concatenate([local, jnp.zeros((LANES - N_SEQ, BLOCK_ROWS), F32)], axis=0).T
    start = jnp.int32(0)
    count = jnp.int32(0)
    for source in range(N_SEQ):
        filled = jnp.sum(jnp.where(rows[source] >= 0, 1.0, 0.0)).astype(jnp.int32)
        plan_out[source] = start
        start = start + (filled + SLOTS - 1) // SLOTS * SLOTS
        count = count + filled
    plan_out[N_SEQ] = (start + ROWS - 1) // ROWS
    count_out[0] = count.astype(F32)


def ranks(owner, lists):
    smem = pl.BlockSpec(memory_space=pltpu.SMEM)
    vmem = pl.BlockSpec(memory_space=pltpu.VMEM)
    return pl.pallas_call(
        rank_kernel,
        out_shape=(
            jax.ShapeDtypeStruct((N_SEQ, BLOCK_ROWS), jnp.int32),
            jax.ShapeDtypeStruct((N_SEQ, BLOCK_ROWS), F32),
            jax.ShapeDtypeStruct((BLOCK_ROWS, LANES), F32),
            jax.ShapeDtypeStruct((N_SEQ + 1,), jnp.int32),
            jax.ShapeDtypeStruct((1,), F32),
        ),
        in_specs=[smem, vmem],
        out_specs=(vmem, vmem, vmem, smem, smem),
        compiler_params=pltpu.CompilerParams(vmem_limit_bytes=8 * 2**20),
        cost_estimate=pl.CostEstimate(flops=10**9, bytes_accessed=10**5, transcendentals=0),
    )(owner, lists)


def arrange_kernel(me, local, context, beyond, rows_out):
    for over, source in enumerate((context, beyond)):
        own = iota((BLOCK_ROWS, LANES), 1) == (me[0] ^ (2 * over))
        column = jnp.sum(jnp.where(own, local[...], 0.0), axis=1, keepdims=True)
        gather = one_hot(column == iota((BLOCK_ROWS, TOK), 1).astype(F32))
        rows_out[over] = mm(gather, source[...]).astype(BF16)


def arrange(me, local, context, beyond):
    smem = pl.BlockSpec(memory_space=pltpu.SMEM)
    vmem = pl.BlockSpec(memory_space=pltpu.VMEM)
    return pl.pallas_call(
        arrange_kernel,
        out_shape=jax.ShapeDtypeStruct((2, BLOCK_ROWS, PRED_WIDTH), BF16),
        in_specs=[smem] + [vmem] * 3,
        out_specs=vmem,
        compiler_params=pltpu.CompilerParams(vmem_limit_bytes=8 * 2**20),
        cost_estimate=pl.CostEstimate(flops=2 * 10**8, bytes_accessed=10**6, transcendentals=0),
    )(me, local, context, beyond)


def predict_kernel(me, lists, *refs):
    pieces = refs[:8]
    gain, w_query, w_key, w_value, hidden_out, context = refs[8:]
    position = me[0]
    for index in range(8):
        for over in range(2):
            source = sender((index % 4) * 4 + over * 2 + index // 4, position)
            rows = pieces[index][over].reshape(N_SEQ, SLOTS, PRED_WIDTH)
            context[:, pl.ds(pl.multiple_of(source * SLOTS, SLOTS), SLOTS), :] = rows

    def block(index, _):
        own = 2 * index + position % 2
        stream = context[own].astype(F32)
        mean = jnp.mean(stream, axis=1, keepdims=True)
        centered = stream - mean
        spread = jnp.mean(centered * centered, axis=1, keepdims=True)
        normed = (centered * lax.rsqrt(spread + 1e-6) * gain[...]).astype(BF16)
        queries = mm(normed, w_query[...]).astype(BF16)
        keys = mm(normed, w_key[...]).astype(BF16)
        values = mm(normed, w_value[...]).astype(BF16)
        key_valid = lists[pl.ds(own, 1), :] >= 0
        ones = jnp.ones((BLOCK_ROWS, LANES), BF16)
        groups = []
        for group in range(PRED_WIDTH // LANES):
            columns = slice(group * LANES, (group + 1) * LANES)
            with_ones = jnp.concatenate([values[:, columns], ones], axis=1)
            total = jnp.zeros((BLOCK_ROWS, LANES), F32)
            sums = jnp.ones((BLOCK_ROWS, LANES), F32)
            for head in range(LANES // PRED_HEAD):
                inside = iota((BLOCK_ROWS, LANES), 1) // PRED_HEAD == head
                masked = jnp.where(inside, queries[:, columns], jnp.zeros((), BF16))
                scores = jnp.where(key_valid, mm_nt(masked, keys[:, columns]), -1e30)
                most = jnp.max(scores, axis=1, keepdims=True)
                weights = jnp.exp2((scores - most) * PRED_SCALE)
                mixed = mm(weights.astype(BF16), with_ones)
                total = jnp.where(inside, mixed[:, :LANES], total)
                sums = jnp.where(inside, mixed[:, LANES:], sums)
            groups.append(total / sums)
        hidden_out[index] = (stream + jnp.concatenate(groups, axis=1)).astype(BF16)
        return 0

    lax.fori_loop(0, N_SEQ // 2, block, 0, unroll=4)


def predict(me, lists, pieces, gain, w_query, w_key, w_value):
    smem = pl.BlockSpec(memory_space=pltpu.SMEM)
    vmem = pl.BlockSpec(memory_space=pltpu.VMEM)
    return pl.pallas_call(
        predict_kernel,
        out_shape=jax.ShapeDtypeStruct((N_SEQ // 2, BLOCK_ROWS, PRED_WIDTH), BF16),
        in_specs=[smem] + [vmem] * 13,
        out_specs=vmem,
        scratch_shapes=[pltpu.VMEM((N_SEQ, BLOCK_ROWS, PRED_WIDTH), BF16)],
        compiler_params=pltpu.CompilerParams(vmem_limit_bytes=16 * 2**20),
        cost_estimate=pl.CostEstimate(flops=13 * 10**9, bytes_accessed=8 * 10**6, transcendentals=10**7),
    )(me, lists, *pieces, gain, w_query, w_key, w_value)


ROWS = 256
TILES = 3
CHUNK = 1024
PACKED = TOKENS + TOK
MIXED = HEAD + 8
STATS = 2 * N_SEQ
LOW, HIGH = 2.0**-80, 2.0**100


def attend_tile(first, extent, key, value_t, packed, result):
    rows = pl.ds(pl.multiple_of(first * ROWS, ROWS), extent)
    query_t = packed[rows, :].astype(F32).T.astype(BF16)
    total = jnp.zeros((MIXED, extent), F32)
    for chunk in range(TOKENS // CHUNK):
        span = slice(chunk * CHUNK, (chunk + 1) * CHUNK)
        weights = jnp.exp2(mm(key[span, :], query_t) * SCALE).astype(BF16)
        total = total + mm(value_t[:MIXED, span], weights)

    def finish(total):
        rest = jnp.zeros((LANES - MIXED, extent), F32)
        mixed = jnp.concatenate([total / total[HEAD : HEAD + 1], rest], axis=0)
        result[rows, :] = mixed.T.astype(BF16)

    finish(total)
    sums = total[HEAD : HEAD + 1]
    safe = (jnp.min(sums) > LOW) & (jnp.max(sums) < HIGH)

    @pl.when(jnp.logical_not(safe))
    def _():
        def peak(chunk, most):
            span = pl.ds(pl.multiple_of(chunk * TOK, TOK), TOK)
            return jnp.maximum(most, jnp.max(mm(key[span, :], query_t), axis=0, keepdims=True))

        most = lax.fori_loop(0, TOKENS // TOK, peak, jnp.full((1, extent), -1e30, F32))

        def mix(chunk, total):
            span = pl.ds(pl.multiple_of(chunk * TOK, TOK), TOK)
            weights = jnp.exp2((mm(key[span, :], query_t) - most) * SCALE).astype(BF16)
            return total + mm(value_t[:MIXED, span], weights)

        finish(lax.fori_loop(0, TOKENS // TOK, mix, jnp.zeros((MIXED, extent), F32)))


def attend_kernel(plan, rank, received, target_out, stats_out, key, value_t, packed, result):
    packed[...] = jnp.zeros((PACKED, LANES), BF16)
    result[...] = jnp.zeros((PACKED, LANES), BF16)
    for source in range(N_SEQ):
        piece = received[source].astype(F32)
        rest = jnp.zeros((LANES - HEAD, TOK), F32)
        span = slice(source * TOK, (source + 1) * TOK)
        key[span, :] = jnp.concatenate([piece[:HEAD], rest], axis=0).T.astype(BF16)
        value_t[:, span] = jnp.concatenate([piece[HEAD : 2 * HEAD], rest + 1.0], axis=0).astype(BF16)
        queries = jnp.concatenate([piece[2 * HEAD :], rest], axis=0).T.astype(BF16)
        packed[pl.ds(pl.multiple_of(plan[source], SLOTS), TOK), :] = queries

    def wide(index, _):
        attend_tile(index * TILES, TILES * ROWS, key, value_t, packed, result)
        return 0

    def narrow(index, _):
        attend_tile(index, ROWS, key, value_t, packed, result)
        return 0

    tiles = plan[N_SEQ]
    lax.fori_loop(0, tiles // TILES, wide, 0)
    lax.fori_loop(tiles // TILES * TILES, tiles, narrow, 0)
    place = iota((TOK, BLOCK_ROWS), 0).astype(F32)
    means, squares = [], []
    for source in range(N_SEQ):
        rows = result[pl.ds(pl.multiple_of(plan[source], SLOTS), TOK), :]
        unpack = one_hot(rank[source : source + 1, :] == place)
        target = lax.dot_general(rows, unpack, (((0,), (0,)), ((), ())), preferred_element_type=F32)[:HEAD]
        target_out[source] = target.astype(BF16)
        mean = jnp.mean(target, axis=0, keepdims=True)
        centered = target - mean
        means.append(mean)
        squares.append(jnp.sum(centered * centered, axis=0, keepdims=True))
    stats = jnp.concatenate(means + squares, axis=0).astype(BF16)
    for other in range(TARGET_HEADS):
        stats_out[other] = stats


def attend(plan, rank, received):
    smem = pl.BlockSpec(memory_space=pltpu.SMEM)
    vmem = pl.BlockSpec(memory_space=pltpu.VMEM)
    return pl.pallas_call(
        attend_kernel,
        out_shape=(
            jax.ShapeDtypeStruct((N_SEQ, HEAD, BLOCK_ROWS), BF16),
            jax.ShapeDtypeStruct((TARGET_HEADS, STATS, BLOCK_ROWS), BF16),
        ),
        in_specs=[smem, vmem, vmem],
        out_specs=(vmem, vmem),
        scratch_shapes=[
            pltpu.VMEM((TOKENS, LANES), BF16),
            pltpu.VMEM((LANES, TOKENS), BF16),
            pltpu.VMEM((PACKED, LANES), BF16),
            pltpu.VMEM((PACKED, LANES), BF16),
        ],
        compiler_params=pltpu.CompilerParams(vmem_limit_bytes=16 * 2**20),
        cost_estimate=pl.CostEstimate(flops=12 * 10**9, bytes_accessed=3 * 10**6, transcendentals=16 * 10**6),
    )(plan, rank, received)


def slot_rows(hidden, source):
    span = slice(source * SLOTS, (source + 1) * SLOTS)
    return hidden[:, span, :].reshape(BLOCK_ROWS, PRED_WIDTH)


def compare_kernel(me, count, rank, target, stats, mine, other, w_proj, slope_out, loss_out, hidden):
    position = me[0]
    for index in range(N_SEQ // 2):
        hidden[2 * index + position % 2] = mine[index]
        hidden[2 * index + 1 - position % 2] = other[index]
    first = position * HEAD
    start = jnp.minimum(first // LANES * LANES, TARGET_WIDTH - WINDOW)
    window = w_proj[:, pl.ds(pl.multiple_of(start, LANES), WINDOW)]
    select = one_hot(iota((HEAD, WINDOW), 1) == iota((HEAD, WINDOW), 0) + (first - start))
    proj = mm_nt(select, window).astype(BF16)
    every = stats[...].astype(F32)
    means = every[:, :N_SEQ]
    mean = jnp.mean(means, axis=0)
    between = means - mean[None]
    spread = (jnp.sum(every[:, N_SEQ:], axis=0) + HEAD * jnp.sum(between * between, axis=0)) / TARGET_WIDTH
    scale = lax.rsqrt(spread + 1e-6)
    keep_all = rank[...] >= 0
    share = 1.0 / jnp.full((1, BLOCK_ROWS), count[0], F32)
    losses = jnp.zeros((HEAD, BLOCK_ROWS), F32)
    for source in range(N_SEQ):
        rows = slot_rows(hidden, source)
        pred = mm_nt(proj, rows)
        one = slice(source, source + 1)
        goal = (target[source].astype(F32) - mean[one]) * scale[one]
        diff = pred - goal
        keep = keep_all[one]
        size = jnp.abs(diff)
        huber = jnp.where(size < 1.0, 0.5 * diff * diff, size - 0.5)
        losses = losses + jnp.where(keep, huber, 0.0)
        slope = jnp.where(keep, jnp.clip(diff, -1.0, 1.0) * share, 0.0)
        slope_out[source] = slope.astype(BF16)
    loss_out[...] = jnp.broadcast_to(jnp.sum(losses), (8, LANES))


def compare(me, count, rank, target, stats, mine, other, w_proj):
    smem = pl.BlockSpec(memory_space=pltpu.SMEM)
    vmem = pl.BlockSpec(memory_space=pltpu.VMEM)
    return pl.pallas_call(
        compare_kernel,
        out_shape=(
            jax.ShapeDtypeStruct((N_SEQ, HEAD, BLOCK_ROWS), BF16),
            jax.ShapeDtypeStruct((8, LANES), F32),
            jax.ShapeDtypeStruct((N_SEQ, BLOCK_ROWS, PRED_WIDTH), BF16),
        ),
        in_specs=[smem, smem] + [vmem] * 6,
        out_specs=(vmem, vmem, vmem),
        compiler_params=pltpu.CompilerParams(vmem_limit_bytes=12 * 2**20),
        cost_estimate=pl.CostEstimate(flops=10**9, bytes_accessed=5 * 10**6, transcendentals=0),
    )(me, count, rank, target, stats, mine, other, w_proj)


def project_kernel(me, lists, slope, hidden, w_proj, grad_out, pred_out):
    key_valid = lists[pl.ds(me[0], 1), :] >= 0
    square = (BLOCK_ROWS, BLOCK_ROWS)
    diagonal = jnp.where(iota(square, 0) == iota(square, 1), jnp.where(key_valid, 1.0, 0.0), 0.0)
    row_valid = jnp.sum(diagonal, axis=1, keepdims=True) > 0.5
    pred_out[...] = jnp.where(row_valid, mm(hidden[me[0]], w_proj[...]), 0.0).astype(BF16)
    gradient = jnp.zeros((HEAD, PRED_WIDTH), F32)
    for source in range(N_SEQ):
        rows = slot_rows(hidden, source)
        gradient = gradient + mm(slope[source], rows)
    rest = jnp.zeros((LANES - HEAD, PRED_WIDTH), F32)
    grad_out[...] = jnp.concatenate([gradient, rest], axis=0).T


def project(me, lists, slope, hidden, w_proj):
    smem = pl.BlockSpec(memory_space=pltpu.SMEM)
    vmem = pl.BlockSpec(memory_space=pltpu.VMEM)
    return pl.pallas_call(
        project_kernel,
        out_shape=(
            jax.ShapeDtypeStruct((PRED_WIDTH, LANES), F32),
            jax.ShapeDtypeStruct((BLOCK_ROWS, TARGET_WIDTH), BF16),
        ),
        in_specs=[smem] + [vmem] * 4,
        out_specs=(vmem, vmem),
        compiler_params=pltpu.CompilerParams(vmem_limit_bytes=8 * 2**20),
        cost_estimate=pl.CostEstimate(flops=4 * 10**9, bytes_accessed=4 * 10**6, transcendentals=0),
    )(me, lists, slope, hidden, w_proj)


def exchange(pieces, axis):
    return lax.all_to_all(pieces, axis, split_axis=0, concat_axis=0, tiled=True)


def across(values, mask):
    return lax.ppermute(values, "seq", [(i, i ^ mask) for i in range(N_SEQ)])


def along(values, step):
    return lax.ppermute(values, "seq", [(i, (i + 4 * step) % N_SEQ) for i in range(N_SEQ)])


def body(
    t_query, t_key, t_value, context, mask_list, block_owner, p_gain, w_query, w_key, w_value, w_proj
):
    me = lax.axis_index("seq").astype(jnp.int32).reshape(1)
    beyond = across(context[0], 2)
    send = pack(me, block_owner, mask_list[0], t_query[0], t_key[0], t_value[0])
    send, beyond = lax.optimization_barrier((send, beyond))
    received = exchange(send, "seq")
    lists, rank, local, plan, count = ranks(block_owner, mask_list[0])
    pair = arrange(me, local, context[0], beyond)
    column = [pair] + [along(pair, step) for step in range(1, 4)]
    pieces = column + [across(part, 1) for part in column]
    hidden = predict(me, lists, pieces, p_gain.reshape(1, PRED_WIDTH), w_query, w_key, w_value)
    received, hidden = lax.optimization_barrier((received, hidden))
    others = across(hidden, 1)
    target, stats = attend(plan, rank, received)
    stats = exchange(stats, "seq")
    slope, loss, rows = compare(me, count, rank, target, stats, hidden, others, w_proj)
    loss, slope = lax.optimization_barrier((loss, slope))
    loss = loss + across(loss, 2)
    gradient, pred_out = project(me, lists, slope, rows, w_proj)
    loss, gradient = lax.optimization_barrier((loss, gradient))
    shares = exchange(gradient.reshape(N_SEQ, PRED_WIDTH // N_SEQ, LANES), "clip")
    for mask in (1, 4, 8):
        loss = loss + across(loss, mask)
    loss = loss[0, :1] / (count * TARGET_WIDTH)
    gradient = jnp.sum(shares, axis=0)[:, :HEAD]
    return (pred_out[None], loss, gradient)


def solution(mesh):
    in_specs = (
        P("clip", "seq", None),
        P("clip", "seq", None),
        P("clip", "seq", None),
        P("clip", "seq", None),
        P("clip", None, None),
        P("clip", None),
        P(),
        P(),
        P(),
        P(),
        P(),
    )
    out_specs = (P("clip", "seq", None), P("clip"), P("clip", "seq"))
    return jax.shard_map(body, mesh=mesh, in_specs=in_specs, out_specs=out_specs, check_vma=False)
```

```python
import math

import jax
import jax.numpy as jnp
from jax import lax
from jax.experimental import pallas as pl
from jax.experimental.pallas import tpu as pltpu
from jax.sharding import PartitionSpec as P

TARGET_WIDTH = 1408
TARGET_HEADS = 16
HEAD = TARGET_WIDTH // TARGET_HEADS
PRED_WIDTH = 384
PRED_HEADS = 12
PRED_HEAD = PRED_WIDTH // PRED_HEADS
BLOCK_ROWS = 256
TOK = 256
N_SEQ = 16
TOKENS = TOK * N_SEQ
SLOTS = BLOCK_ROWS // N_SEQ
WINDOW = 256
LANES = 128
PIECE = 3 * HEAD
SCALE = math.log2(math.e) / math.sqrt(HEAD)
PRED_SCALE = math.log2(math.e) / math.sqrt(PRED_HEAD)

BF16 = jnp.bfloat16
F32 = jnp.float32


def mm(a, b):
    return jnp.dot(a, b, preferred_element_type=F32)


def mm_nt(a, b):
    return lax.dot_general(a, b, (((1,), (1,)), ((), ())), preferred_element_type=F32)


def iota(shape, dim):
    return lax.broadcasted_iota(jnp.int32, shape, dim)


def one_hot(mask):
    return jnp.where(mask, 1.0, 0.0).astype(BF16)


def spread_row(values, source):
    pick = one_hot(iota((BLOCK_ROWS, BLOCK_ROWS), 0) == source * SLOTS + iota((BLOCK_ROWS, BLOCK_ROWS), 1) % SLOTS)
    wide = mm(values.astype(BF16), pick)
    own = iota((N_SEQ, BLOCK_ROWS), 1) // SLOTS == iota((N_SEQ, BLOCK_ROWS), 0)
    return jnp.sum(jnp.where(own, wide, 0.0), axis=0, keepdims=True)


def earlier():
    return one_hot(iota((BLOCK_ROWS, BLOCK_ROWS), 0) < iota((BLOCK_ROWS, BLOCK_ROWS), 1))


def head_columns(head):
    start = min(head * HEAD // LANES * LANES, TARGET_WIDTH - WINDOW)
    return start, head * HEAD - start


def sender(piece, position):
    step = (position // 4 + 4 - piece // 4) % 4
    return step * 4 + ((position % 4) ^ (piece % 4))


def pack_kernel(me, owner, lists_in, query_in, keys_in, values_in, send, lists, blocks, query, keys, values, sems):
    loads = [
        pltpu.make_async_copy(source, place, sems.at[i])
        for i, (source, place) in enumerate(
            [(lists_in, lists), (keys_in, keys), (values_in, values), (query_in, query)]
        )
    ]
    for load in loads:
        load.start()
    position = me[0]
    loads[0].wait()
    for b in range(N_SEQ):
        blocks[pl.ds(owner[0, b], 1), :] = lists[b : b + 1, :]
    ordered = blocks[...]
    row = spread_row(jnp.where(ordered >= 0, ordered - position * TOK, -1).astype(F32), position)
    valid = jnp.broadcast_to(row >= 0, (8, BLOCK_ROWS))
    rank = mm(one_hot(valid), earlier())[0:1]
    rank = jnp.where(row >= 0, rank, -1.0)
    place = iota((BLOCK_ROWS, BLOCK_ROWS), 0).astype(F32)
    compact = mm_nt(one_hot(rank == place), one_hot(row == place)).astype(BF16)
    for load in loads[1:]:
        load.wait()
    packed_query = mm(compact, query[...]).astype(BF16)
    for head in range(TARGET_HEADS):
        start, offset = head_columns(head)
        select = one_hot(iota((HEAD, WINDOW), 1) == iota((HEAD, WINDOW), 0) + offset)
        parts = [
            mm_nt(select, keys[:, start : start + WINDOW]),
            mm_nt(select, values[:, start : start + WINDOW]),
            mm_nt(select, packed_query[:, start : start + WINDOW]),
        ]
        send[head] = jnp.concatenate(parts, axis=0).astype(BF16)


def pack(me, owner, lists, query, keys, values):
    smem = pl.BlockSpec(memory_space=pltpu.SMEM)
    vmem = pl.BlockSpec(memory_space=pltpu.VMEM)
    hbm = pl.BlockSpec(memory_space=pltpu.HBM)
    return pl.pallas_call(
        pack_kernel,
        out_shape=jax.ShapeDtypeStruct((TARGET_HEADS, PIECE, TOK), BF16),
        in_specs=[smem, smem] + [hbm] * 4,
        out_specs=vmem,
        scratch_shapes=[
            pltpu.VMEM((N_SEQ, BLOCK_ROWS), jnp.int32),
            pltpu.VMEM((N_SEQ, BLOCK_ROWS), jnp.int32),
            pltpu.VMEM((TOK, TARGET_WIDTH), BF16),
            pltpu.VMEM((TOK, TARGET_WIDTH), BF16),
            pltpu.VMEM((TOK, TARGET_WIDTH), BF16),
            pltpu.SemaphoreType.DMA((4,)),
        ],
        compiler_params=pltpu.CompilerParams(vmem_limit_bytes=56 * 2**20),
        cost_estimate=pl.CostEstimate(flops=3 * 10**9, bytes_accessed=5 * 10**6, transcendentals=0),
    )(me, owner, lists, query, keys, values)


def rank_kernel(owner, lists, lists_out, rank_out, local_out, plan_out, count_out):
    for b in range(N_SEQ):
        lists_out[pl.ds(owner[0, b], 1), :] = lists[b : b + 1, :]
    ordered = lists_out[...]
    rows = []
    for source in range(N_SEQ):
        local = jnp.where(ordered >= 0, ordered - source * TOK, -1).astype(F32)
        rows.append(spread_row(local, source))
    local = jnp.concatenate(rows, axis=0)
    rank_out[...] = jnp.where(local >= 0, mm(one_hot(local >= 0), earlier()), -1.0)
    local_out[...] = jnp.concatenate([local, jnp.zeros((LANES - N_SEQ, BLOCK_ROWS), F32)], axis=0).T
    start = jnp.int32(0)
    count = jnp.int32(0)
    for source in range(N_SEQ):
        filled = jnp.sum(jnp.where(rows[source] >= 0, 1.0, 0.0)).astype(jnp.int32)
        plan_out[source] = start
        start = start + (filled + SLOTS - 1) // SLOTS * SLOTS
        count = count + filled
    plan_out[N_SEQ] = (start + ROWS - 1) // ROWS
    count_out[0] = count.astype(F32)


def ranks(owner, lists):
    smem = pl.BlockSpec(memory_space=pltpu.SMEM)
    vmem = pl.BlockSpec(memory_space=pltpu.VMEM)
    return pl.pallas_call(
        rank_kernel,
        out_shape=(
            jax.ShapeDtypeStruct((N_SEQ, BLOCK_ROWS), jnp.int32),
            jax.ShapeDtypeStruct((N_SEQ, BLOCK_ROWS), F32),
            jax.ShapeDtypeStruct((BLOCK_ROWS, LANES), F32),
            jax.ShapeDtypeStruct((N_SEQ + 1,), jnp.int32),
            jax.ShapeDtypeStruct((1,), F32),
        ),
        in_specs=[smem, vmem],
        out_specs=(vmem, vmem, vmem, smem, smem),
        compiler_params=pltpu.CompilerParams(vmem_limit_bytes=8 * 2**20),
        cost_estimate=pl.CostEstimate(flops=10**9, bytes_accessed=10**5, transcendentals=0),
    )(owner, lists)


def arrange_kernel(me, local, context, beyond, rows_out):
    for over, source in enumerate((context, beyond)):
        own = iota((BLOCK_ROWS, LANES), 1) == (me[0] ^ (2 * over))
        column = jnp.sum(jnp.where(own, local[...], 0.0), axis=1, keepdims=True)
        gather = one_hot(column == iota((BLOCK_ROWS, TOK), 1).astype(F32))
        rows_out[over] = mm(gather, source[...]).astype(BF16)


def arrange(me, local, context, beyond):
    smem = pl.BlockSpec(memory_space=pltpu.SMEM)
    vmem = pl.BlockSpec(memory_space=pltpu.VMEM)
    return pl.pallas_call(
        arrange_kernel,
        out_shape=jax.ShapeDtypeStruct((2, BLOCK_ROWS, PRED_WIDTH), BF16),
        in_specs=[smem] + [vmem] * 3,
        out_specs=vmem,
        compiler_params=pltpu.CompilerParams(vmem_limit_bytes=8 * 2**20),
        cost_estimate=pl.CostEstimate(flops=2 * 10**8, bytes_accessed=10**6, transcendentals=0),
    )(me, local, context, beyond)


def predict_kernel(me, lists, *refs):
    pieces = refs[:8]
    gain, w_query, w_key, w_value, hidden_out, context = refs[8:]
    position = me[0]
    for index in range(8):
        for over in range(2):
            source = sender((index % 4) * 4 + over * 2 + index // 4, position)
            rows = pieces[index][over].reshape(N_SEQ, SLOTS, PRED_WIDTH)
            context[:, pl.ds(pl.multiple_of(source * SLOTS, SLOTS), SLOTS), :] = rows

    def block(index, _):
        own = 2 * index + position % 2
        stream = context[own].astype(F32)
        mean = jnp.mean(stream, axis=1, keepdims=True)
        centered = stream - mean
        spread = jnp.mean(centered * centered, axis=1, keepdims=True)
        normed = (centered * lax.rsqrt(spread + 1e-6) * gain[...]).astype(BF16)
        queries = mm(normed, w_query[...]).astype(BF16)
        keys = mm(normed, w_key[...]).astype(BF16)
        values = mm(normed, w_value[...]).astype(BF16)
        key_valid = lists[pl.ds(own, 1), :] >= 0
        ones = jnp.ones((BLOCK_ROWS, LANES), BF16)
        groups = []
        for group in range(PRED_WIDTH // LANES):
            columns = slice(group * LANES, (group + 1) * LANES)
            with_ones = jnp.concatenate([values[:, columns], ones], axis=1)
            total = jnp.zeros((BLOCK_ROWS, LANES), F32)
            sums = jnp.ones((BLOCK_ROWS, LANES), F32)
            for head in range(LANES // PRED_HEAD):
                inside = iota((BLOCK_ROWS, LANES), 1) // PRED_HEAD == head
                masked = jnp.where(inside, queries[:, columns], jnp.zeros((), BF16))
                scores = jnp.where(key_valid, mm_nt(masked, keys[:, columns]), -1e30)
                most = jnp.max(scores, axis=1, keepdims=True)
                weights = jnp.exp2((scores - most) * PRED_SCALE)
                mixed = mm(weights.astype(BF16), with_ones)
                total = jnp.where(inside, mixed[:, :LANES], total)
                sums = jnp.where(inside, mixed[:, LANES:], sums)
            groups.append(total / sums)
        hidden_out[index] = (stream + jnp.concatenate(groups, axis=1)).astype(BF16)
        return 0

    lax.fori_loop(0, N_SEQ // 2, block, 0, unroll=4)


def predict(me, lists, pieces, gain, w_query, w_key, w_value):
    smem = pl.BlockSpec(memory_space=pltpu.SMEM)
    vmem = pl.BlockSpec(memory_space=pltpu.VMEM)
    return pl.pallas_call(
        predict_kernel,
        out_shape=jax.ShapeDtypeStruct((N_SEQ // 2, BLOCK_ROWS, PRED_WIDTH), BF16),
        in_specs=[smem] + [vmem] * 13,
        out_specs=vmem,
        scratch_shapes=[pltpu.VMEM((N_SEQ, BLOCK_ROWS, PRED_WIDTH), BF16)],
        compiler_params=pltpu.CompilerParams(vmem_limit_bytes=16 * 2**20),
        cost_estimate=pl.CostEstimate(flops=13 * 10**9, bytes_accessed=8 * 10**6, transcendentals=10**7),
    )(me, lists, *pieces, gain, w_query, w_key, w_value)


ROWS = 256
TILES = 3
CHUNK = 1024
PACKED = TOKENS + TOK
MIXED = HEAD + 8
STATS = 2 * N_SEQ
LOW, HIGH = 2.0**-80, 2.0**100


def attend_tile(first, extent, key, value_t, packed, result):
    rows = pl.ds(pl.multiple_of(first * ROWS, ROWS), extent)
    query_t = packed[rows, :].astype(F32).T.astype(BF16)
    total = jnp.zeros((MIXED, extent), F32)
    for chunk in range(TOKENS // CHUNK):
        span = slice(chunk * CHUNK, (chunk + 1) * CHUNK)
        weights = jnp.exp2(mm(key[span, :], query_t) * SCALE).astype(BF16)
        total = total + mm(value_t[:MIXED, span], weights)

    def finish(total):
        rest = jnp.zeros((LANES - MIXED, extent), F32)
        mixed = jnp.concatenate([total / total[HEAD : HEAD + 1], rest], axis=0)
        result[rows, :] = mixed.T.astype(BF16)

    finish(total)
    sums = total[HEAD : HEAD + 1]
    safe = (jnp.min(sums) > LOW) & (jnp.max(sums) < HIGH)

    @pl.when(jnp.logical_not(safe))
    def _():
        def peak(chunk, most):
            span = pl.ds(pl.multiple_of(chunk * TOK, TOK), TOK)
            return jnp.maximum(most, jnp.max(mm(key[span, :], query_t), axis=0, keepdims=True))

        most = lax.fori_loop(0, TOKENS // TOK, peak, jnp.full((1, extent), -1e30, F32))

        def mix(chunk, total):
            span = pl.ds(pl.multiple_of(chunk * TOK, TOK), TOK)
            weights = jnp.exp2((mm(key[span, :], query_t) - most) * SCALE).astype(BF16)
            return total + mm(value_t[:MIXED, span], weights)

        finish(lax.fori_loop(0, TOKENS // TOK, mix, jnp.zeros((MIXED, extent), F32)))


def attend_kernel(plan, rank, received, target_out, stats_out, key, value_t, packed, result):
    packed[...] = jnp.zeros((PACKED, LANES), BF16)
    result[...] = jnp.zeros((PACKED, LANES), BF16)
    for source in range(N_SEQ):
        piece = received[source].astype(F32)
        rest = jnp.zeros((LANES - HEAD, TOK), F32)
        span = slice(source * TOK, (source + 1) * TOK)
        key[span, :] = jnp.concatenate([piece[:HEAD], rest], axis=0).T.astype(BF16)
        value_t[:, span] = jnp.concatenate([piece[HEAD : 2 * HEAD], rest + 1.0], axis=0).astype(BF16)
        queries = jnp.concatenate([piece[2 * HEAD :], rest], axis=0).T.astype(BF16)
        packed[pl.ds(pl.multiple_of(plan[source], SLOTS), TOK), :] = queries

    def wide(index, _):
        attend_tile(index * TILES, TILES * ROWS, key, value_t, packed, result)
        return 0

    tiles = plan[N_SEQ]
    done = tiles // TILES * TILES

    def double(_, carry):
        attend_tile(done, 2 * ROWS, key, value_t, packed, result)
        return carry

    def narrow(_, carry):
        attend_tile(done, ROWS, key, value_t, packed, result)
        return carry

    lax.fori_loop(0, tiles // TILES, wide, 0)
    rest_tiles = tiles % TILES
    lax.fori_loop(0, rest_tiles // 2, double, 0)
    lax.fori_loop(0, rest_tiles % 2, narrow, 0)
    place = iota((TOK, BLOCK_ROWS), 0).astype(F32)
    means, squares = [], []
    for source in range(N_SEQ):
        rows = result[pl.ds(pl.multiple_of(plan[source], SLOTS), TOK), :]
        unpack = one_hot(rank[source : source + 1, :] == place)
        target = lax.dot_general(rows, unpack, (((0,), (0,)), ((), ())), preferred_element_type=F32)[:HEAD]
        target_out[source] = target.astype(BF16)
        mean = jnp.mean(target, axis=0, keepdims=True)
        centered = target - mean
        means.append(mean)
        squares.append(jnp.sum(centered * centered, axis=0, keepdims=True))
    stats = jnp.concatenate(means + squares, axis=0).astype(BF16)
    for other in range(TARGET_HEADS):
        stats_out[other] = stats


def attend(plan, rank, received):
    smem = pl.BlockSpec(memory_space=pltpu.SMEM)
    vmem = pl.BlockSpec(memory_space=pltpu.VMEM)
    return pl.pallas_call(
        attend_kernel,
        out_shape=(
            jax.ShapeDtypeStruct((N_SEQ, HEAD, BLOCK_ROWS), BF16),
            jax.ShapeDtypeStruct((TARGET_HEADS, STATS, BLOCK_ROWS), BF16),
        ),
        in_specs=[smem, vmem, vmem],
        out_specs=(vmem, vmem),
        scratch_shapes=[
            pltpu.VMEM((TOKENS, LANES), BF16),
            pltpu.VMEM((LANES, TOKENS), BF16),
            pltpu.VMEM((PACKED, LANES), BF16),
            pltpu.VMEM((PACKED, LANES), BF16),
        ],
        compiler_params=pltpu.CompilerParams(vmem_limit_bytes=16 * 2**20),
        cost_estimate=pl.CostEstimate(flops=12 * 10**9, bytes_accessed=3 * 10**6, transcendentals=16 * 10**6),
    )(plan, rank, received)


def slot_rows(hidden, source):
    span = slice(source * SLOTS, (source + 1) * SLOTS)
    return hidden[:, span, :].reshape(BLOCK_ROWS, PRED_WIDTH)


def compare_kernel(me, count, rank, target, stats, mine, other, w_proj, slope_out, loss_out, hidden):
    position = me[0]
    for index in range(N_SEQ // 2):
        hidden[2 * index + position % 2] = mine[index]
        hidden[2 * index + 1 - position % 2] = other[index]
    first = position * HEAD
    start = jnp.minimum(first // LANES * LANES, TARGET_WIDTH - WINDOW)
    window = w_proj[:, pl.ds(pl.multiple_of(start, LANES), WINDOW)]
    select = one_hot(iota((HEAD, WINDOW), 1) == iota((HEAD, WINDOW), 0) + (first - start))
    proj = mm_nt(select, window).astype(BF16)
    every = stats[...].astype(F32)
    means = every[:, :N_SEQ]
    mean = jnp.mean(means, axis=0)
    between = means - mean[None]
    spread = (jnp.sum(every[:, N_SEQ:], axis=0) + HEAD * jnp.sum(between * between, axis=0)) / TARGET_WIDTH
    scale = lax.rsqrt(spread + 1e-6)
    keep_all = rank[...] >= 0
    share = 1.0 / jnp.full((1, BLOCK_ROWS), count[0], F32)
    losses = jnp.zeros((HEAD, BLOCK_ROWS), F32)
    for source in range(N_SEQ):
        rows = slot_rows(hidden, source)
        pred = mm_nt(proj, rows)
        one = slice(source, source + 1)
        goal = (target[source].astype(F32) - mean[one]) * scale[one]
        diff = pred - goal
        keep = keep_all[one]
        size = jnp.abs(diff)
        huber = jnp.where(size < 1.0, 0.5 * diff * diff, size - 0.5)
        losses = losses + jnp.where(keep, huber, 0.0)
        slope = jnp.where(keep, jnp.clip(diff, -1.0, 1.0) * share, 0.0)
        slope_out[source] = slope.astype(BF16)
    loss_out[...] = jnp.broadcast_to(jnp.sum(losses), (8, LANES))


def compare(me, count, rank, target, stats, mine, other, w_proj):
    smem = pl.BlockSpec(memory_space=pltpu.SMEM)
    vmem = pl.BlockSpec(memory_space=pltpu.VMEM)
    return pl.pallas_call(
        compare_kernel,
        out_shape=(
            jax.ShapeDtypeStruct((N_SEQ, HEAD, BLOCK_ROWS), BF16),
            jax.ShapeDtypeStruct((8, LANES), F32),
            jax.ShapeDtypeStruct((N_SEQ, BLOCK_ROWS, PRED_WIDTH), BF16),
        ),
        in_specs=[smem, smem] + [vmem] * 6,
        out_specs=(vmem, vmem, vmem),
        compiler_params=pltpu.CompilerParams(vmem_limit_bytes=12 * 2**20),
        cost_estimate=pl.CostEstimate(flops=10**9, bytes_accessed=5 * 10**6, transcendentals=0),
    )(me, count, rank, target, stats, mine, other, w_proj)


def project_kernel(me, lists, slope, hidden, w_proj, grad_out, pred_out):
    key_valid = lists[pl.ds(me[0], 1), :] >= 0
    square = (BLOCK_ROWS, BLOCK_ROWS)
    diagonal = jnp.where(iota(square, 0) == iota(square, 1), jnp.where(key_valid, 1.0, 0.0), 0.0)
    row_valid = jnp.sum(diagonal, axis=1, keepdims=True) > 0.5
    pred_out[...] = jnp.where(row_valid, mm(hidden[me[0]], w_proj[...]), 0.0).astype(BF16)
    gradient = jnp.zeros((HEAD, PRED_WIDTH), F32)
    for source in range(N_SEQ):
        rows = slot_rows(hidden, source)
        gradient = gradient + mm(slope[source], rows)
    rest = jnp.zeros((LANES - HEAD, PRED_WIDTH), F32)
    grad_out[...] = jnp.concatenate([gradient, rest], axis=0).T


def project(me, lists, slope, hidden, w_proj):
    smem = pl.BlockSpec(memory_space=pltpu.SMEM)
    vmem = pl.BlockSpec(memory_space=pltpu.VMEM)
    return pl.pallas_call(
        project_kernel,
        out_shape=(
            jax.ShapeDtypeStruct((PRED_WIDTH, LANES), F32),
            jax.ShapeDtypeStruct((BLOCK_ROWS, TARGET_WIDTH), BF16),
        ),
        in_specs=[smem] + [vmem] * 4,
        out_specs=(vmem, vmem),
        compiler_params=pltpu.CompilerParams(vmem_limit_bytes=8 * 2**20),
        cost_estimate=pl.CostEstimate(flops=4 * 10**9, bytes_accessed=4 * 10**6, transcendentals=0),
    )(me, lists, slope, hidden, w_proj)


def exchange(pieces, axis):
    return lax.all_to_all(pieces, axis, split_axis=0, concat_axis=0, tiled=True)


def across(values, mask):
    return lax.ppermute(values, "seq", [(i, i ^ mask) for i in range(N_SEQ)])


def along(values, step):
    return lax.ppermute(values, "seq", [(i, (i + 4 * step) % N_SEQ) for i in range(N_SEQ)])


def body(
    t_query, t_key, t_value, context, mask_list, block_owner, p_gain, w_query, w_key, w_value, w_proj
):
    me = lax.axis_index("seq").astype(jnp.int32).reshape(1)
    beyond = across(context[0], 2)
    send = pack(me, block_owner, mask_list[0], t_query[0], t_key[0], t_value[0])
    send, beyond = lax.optimization_barrier((send, beyond))
    received = exchange(send, "seq")
    lists, rank, local, plan, count = ranks(block_owner, mask_list[0])
    pair = arrange(me, local, context[0], beyond)
    column = [pair] + [along(pair, step) for step in range(1, 4)]
    pieces = column + [across(part, 1) for part in column]
    hidden = predict(me, lists, pieces, p_gain.reshape(1, PRED_WIDTH), w_query, w_key, w_value)
    received, hidden = lax.optimization_barrier((received, hidden))
    others = across(hidden, 1)
    target, stats = attend(plan, rank, received)
    stats = exchange(stats, "seq")
    slope, loss, rows = compare(me, count, rank, target, stats, hidden, others, w_proj)
    loss, slope = lax.optimization_barrier((loss, slope))
    loss = loss + across(loss, 2)
    gradient, pred_out = project(me, lists, slope, rows, w_proj)
    loss, gradient = lax.optimization_barrier((loss, gradient))
    shares = exchange(gradient.reshape(N_SEQ, PRED_WIDTH // N_SEQ, LANES), "clip")
    for mask in (1, 4, 8):
        loss = loss + across(loss, mask)
    loss = loss[0, :1] / (count * TARGET_WIDTH)
    gradient = jnp.sum(shares, axis=0)[:, :HEAD]
    return (pred_out[None], loss, gradient)


def solution(mesh):
    in_specs = (
        P("clip", "seq", None),
        P("clip", "seq", None),
        P("clip", "seq", None),
        P("clip", "seq", None),
        P("clip", None, None),
        P("clip", None),
        P(),
        P(),
        P(),
        P(),
        P(),
    )
    out_specs = (P("clip", "seq", None), P("clip"), P("clip", "seq"))
    return jax.shard_map(body, mesh=mesh, in_specs=in_specs, out_specs=out_specs, check_vma=False)
```
